512 devices in a mesh: dp: 128 (over z, y, core), cent: 4 (over x).
Axes of the slice: x: 4, y: 8, z: 8, core: 2. Of those that a mesh axis runs over, the one named last changes fastest.
Arguments:
- embeddings: float32 [131072, 768], P(('dp', 'cent')), may hold values from -6 to 6
- assignment: int32 [131072, 1], P(('dp', 'cent')), may hold values from 0 to 255; in each aligned block of 256 rows (0 to 255, 256 to 511, ...) at most 2 rows name the same one
- slab_ids: int32 [256], replicated, may hold values from 0 to 65535, as said below
- centroids: float32 [65536, 768], P(('dp', 'cent')), may hold values from -0.21875 to 0.21875
Outputs:
- new_table: float32 [65536, 768], P(('dp', 'cent'))
- centroid_cos: float32 [131072], P(('dp', 'cent'))
- max_sim: float32 [131072], P(('dp', 'cent'))
The draws below stay inside these ranges and needn't reach their ends.
Inputs may be any that keep to these rules, and one draw needn't show every extreme that they name: `slab_ids`: distinct table rows. `assignment`: among the 256 rows of one device (aligned blocks) no cluster is named by more than 2 rows, a bound that some block reaches; every cluster has at least one row.
All inputs are finite; a program needn't handle non-finite values.
Results may differ from the reference program's by a relative error of at most 0.0003.
Values sent between devices are 32-bit elements; how exact they have to be, the bound alone decides.
A program may use at most 64 MiB of HBM per device.

```python
import math
import jax
import jax.numpy as jnp
import numpy as np
from jax import lax

E = 768
ROW_DEV = 256
CENTROIDS = 65536
SLAB = 256
CAP_C = 2
ROWS = 131072
DEVICES = 512


def draw_slab_ids(key, part):
    key = jax.random.fold_in(key, 5)
    return jax.random.permutation(key, CENTROIDS)[:SLAB].astype(jnp.int32)


def levels(own_key, extent, shards, low, largest):
    def one(axis_at, shards_of):
        steps = jax.random.uniform(jax.random.fold_in(jax.random.fold_in(own_key, 6), axis_at), (shards_of,), jnp.float32, low / len(shards), largest / len(shards))
        return jnp.repeat(jnp.exp(steps), extent[axis_at] // shards_of).reshape((-1,) + (1,) * (len(extent) - axis_at - 1))

    factor_of = one(*shards[0])
    for cut in shards[1:]:
        factor_of = factor_of * one(*cut)
    return factor_of


def routed_block(key, own, number, rows, count, top, most, skew):
    order = jax.random.permutation(key, count)
    crowded, usual = load_shares(count, rows * top, most, skew, True), load_shares(count, rows * top, most, skew, False)
    places = jnp.arange(count)

    def named(lengths, turn):
        used = int((lengths > 0).sum())
        fixed = max(1, used // 4)
        shifted = fixed + (places - fixed + turn * (used - fixed)) % max(1, count - fixed)
        return jnp.zeros((count,), jnp.int32).at[order[jnp.where(places < fixed, places, shifted)]].set(jnp.asarray(lengths, jnp.int32))

    lengths = jnp.where(number % 4 == 0, named(crowded, number // 4), named(usual, number - number // 4 - 1))
    mixed = jax.random.permutation(jax.random.fold_in(own, 3), count)
    giver, receiver = mixed[0:count // 2 * 2:2], mixed[1:count // 2 * 2:2]
    slack = jnp.minimum(lengths[giver] - 1, most - lengths[receiver]) // 2
    slack = jnp.where((giver == order[0]) | (receiver == order[0]) | (lengths[receiver] == 0), 0, jnp.maximum(slack, 0))
    shifted = jax.random.randint(jax.random.fold_in(own, 4), (count // 2,), 0, 1 << 20) % (slack + 1)
    lengths = lengths.at[giver].add(-shifted).at[receiver].add(shifted)
    members = jnp.searchsorted(jnp.cumsum(lengths), jnp.arange(rows * top), side="right").astype(jnp.int32)
    table = members.reshape(top, rows).T
    table = table[jax.random.permutation(jax.random.fold_in(own, 1), rows)]
    turn = jax.random.randint(jax.random.fold_in(own, 2), (rows, 1), 0, top)
    return jnp.take_along_axis(table, (jnp.arange(top)[None, :] + turn) % top, axis=1)


def load_shares(number_of, total, limit, slope, full):
    portions = [(1 << 20) // math.isqrt(rank ** slope) + 1 for rank in range(1, number_of + 1)]
    largest = limit if full else min(limit, max(-(-total // number_of), total * portions[0] // sum(portions)))
    least = 1 if total - largest >= number_of - 1 else 0
    given, spare = [largest] + [least] * (number_of - 1), total - largest - least * (number_of - 1)
    while spare > 0:
        candidates = [i for i in range(1, number_of) if given[i] < largest] or [i for i in range(1, number_of) if given[i] < limit]
        mass, budget = sum([portions[i] for i in candidates]), spare
        for i in candidates:
            extra = min(limit - given[i], max(1, budget * portions[i] // mass), spare)
            given[i] = given[i] + extra
            spare = spare - extra
    return np.array(given)


def scatter_about(rng, extent, deviation, bound, shards=(), held_as=jnp.bfloat16):
    loudness = levels(rng, extent, shards, -0.22, 0.18) if shards else 1.0
    drawn = jax.random.normal(rng, extent, jnp.float32) * deviation * loudness
    return jnp.minimum(jnp.maximum(drawn, -bound), bound).astype(held_as)


def setup_inputs(seed: int = 0) -> dict:
    key_of = jax.random.split(jax.random.key(seed), 5)
    embeddings = scatter_about(key_of[0], (ROWS, E), 1.0, 6.0, ((0, 512),), jnp.float32)
    assignment_keys = jax.random.split(jax.random.fold_in(key_of[1], 1), ROWS // ROW_DEV)
    assignment_turns = jax.random.permutation(jax.random.fold_in(key_of[1], 3), ROWS // ROW_DEV)
    assignment = jax.vmap(lambda own, number: routed_block(jax.random.fold_in(key_of[1], 2), own, number, ROW_DEV, SLAB, 1, CAP_C, 2))(assignment_keys, assignment_turns).reshape((ROWS, 1))
    slab_ids = draw_slab_ids(jax.random.fold_in(key_of[4], 71), 0)
    centroids = scatter_about(key_of[3], (CENTROIDS, E), E ** -0.5, 0.21875, ((0, 512),), jnp.float32)
    return dict(embeddings=embeddings, assignment=assignment, slab_ids=slab_ids, centroids=centroids)


epsilon = 1e-06

def normalize(values):
    return values * lax.rsqrt(lax.optimization_barrier(jnp.sum(values * values, axis=-1, keepdims=True)) + epsilon)

def reference(embeddings, assignment, slab_ids, centroids):
    unit = normalize(embeddings)
    labels = assignment[:, 0].astype(jnp.int32)
    sums = jax.ops.segment_sum(unit, labels, num_segments=SLAB)
    fresh = normalize(sums)
    new_table = centroids.at[slab_ids].set(fresh)
    centroid_cos = lax.optimization_barrier(jnp.sum(unit * fresh[labels], axis=1))
    order = jnp.argsort(labels, stable=True).astype(jnp.int32)
    sorted_unit = unit[order]
    sorted_labels = labels[order]
    counts = jnp.zeros((SLAB,), jnp.int32).at[labels].add(1)
    starts = (jnp.cumsum(counts) - counts).astype(jnp.int32)
    biggest = CAP_C * DEVICES
    padded = jnp.concatenate([sorted_unit, jnp.zeros((biggest, E), jnp.float32)], axis=0)

    def one_cluster(cluster):
        start = starts[cluster]
        block = lax.dynamic_slice(padded, (start, jnp.int32(0)), (biggest, E))
        sims = jnp.dot(block, block.T, precision=lax.Precision.HIGHEST, preferred_element_type=jnp.float32)
        index = jnp.arange(biggest, dtype=jnp.int32)
        usable = (index[None, :] < counts[cluster]) & (index[:, None] != index[None, :])
        masked = jnp.where(usable, sims, jnp.float32(-2.0))
        return jnp.maximum(lax.optimization_barrier(jnp.max(masked, axis=1)), jnp.float32(-1.0))
    results = lax.map(one_cluster, jnp.arange(SLAB, dtype=jnp.int32))
    place = jnp.arange(ROWS, dtype=jnp.int32) - starts[sorted_labels]
    sorted_best = results[sorted_labels, place]
    max_sim = jnp.zeros((ROWS,), jnp.float32).at[order].set(sorted_best)
    return (new_table, centroid_cos, max_sim)
```

```python
import functools

import jax
import jax.numpy as jnp
from jax import lax
from jax.experimental import pallas as pl
from jax.experimental.pallas import tpu as pltpu
from jax.sharding import PartitionSpec as P

epsilon = 1e-06
Z, Y, X = 8, 8, 4
GROUP = 8
SENTINEL = 4.0
MESH = pl.DeviceIdType.MESH
f32, bf16 = jnp.float32, jnp.bfloat16


def split3(v):
    hi = v.astype(bf16)
    rest = v - hi.astype(f32)
    mid = rest.astype(bf16)
    lo = (rest - mid.astype(f32)).astype(bf16)
    return hi, mid, lo


def select_rows(onehot, v):
    hi, mid, lo = split3(v)
    dot = functools.partial(jnp.dot, preferred_element_type=f32)
    return dot(onehot, hi) + dot(onehot, mid) + dot(onehot, lo)


def dot_nt(a, b):
    return lax.dot_general(a, b, (((1,), (1,)), ((), ())), preferred_element_type=f32)


def iota(shape, axis):
    return lax.broadcasted_iota(jnp.int32, shape, axis)


def kernel(dims, emb, lab, slab, cent, table, cos_out, sim_out,
           send, recv, other, khi, klo, bias, frow, fpart, abuf, ans,
           line_sem, plane_sem, own_sem,
           fs, fr, ps, pr, ns, nr, xs_, xr, cs, cr, as_, ar, bs, br):
    Z, Y, X = dims
    nyz = Z * Y
    chips = nyz * X
    n_group = nyz // GROUP
    rows, width = emb.shape
    tiles = width // 128
    half_t = tiles // 2
    msg = 2 * tiles
    own = 2 * chips

    dp = lax.axis_index("dp")
    x = lax.axis_index("cent")
    core = dp % 2
    yz = dp // 2
    y = yz % Y
    z = yz // Y
    me = x * nyz + yz

    def device(zz, yy, xx, cc):
        return ((zz * Y + yy) * 2 + cc, xx)

    barrier = pltpu.get_barrier_semaphore()

    def signal(sem, zz, yy, xx, cc):
        pl.semaphore_signal(sem, inc=1, device_id=device(zz, yy, xx, cc), device_id_type=MESH)

    for d in range(1, Z):
        signal(barrier, (z + d) % Z, y, x, core)
    for d in range(1, Y):
        signal(barrier, z, (y + d) % Y, x, core)
    for d in range(1, X):
        signal(barrier, z, y, (x + d) % X, core)
    signal(barrier, z, y, x, 1 - core)

    e = emb[...]
    unit = e * lax.rsqrt(jnp.sum(e * e, axis=1, keepdims=True) + epsilon)

    pl.semaphore_wait(barrier, Z + Y + X - 2)
    for d in range(1, Y):
        signal(line_sem, z, (y + d) % Y, x, core)

    lrow = lab[...]
    lcol = jnp.broadcast_to(lrow.astype(f32), (128, rows)).T[:, 0:1].astype(jnp.int32)
    earlier = (lcol == lrow) & (iota((rows, rows), 0) < iota((rows, rows), 1))
    rank = jnp.sum(jnp.where(earlier, 1.0, 0.0), axis=0, keepdims=True).astype(jnp.int32)
    target = 2 * lrow + rank
    place = jnp.where(iota((own, rows), 0) == target, 1.0, 0.0)
    filled = jnp.sum(place, axis=1, keepdims=True) > 0.5
    slots = select_rows(place.astype(bf16), unit)
    slots = jnp.where(filled, slots, SENTINEL)
    for t in range(tiles):
        send[pl.ds(t, own, stride=tiles), :] = slots[:, t * 128:(t + 1) * 128]

    pl.semaphore_wait(line_sem, Y - 1)
    for d in range(1, X):
        signal(plane_sem, z, y, (x + d) % X, core)
    pl.semaphore_wait(plane_sem, X - 1)

    def offset(q):
        w = (q * 37) % nyz
        return w // Y, w % Y

    def forward(q, dx, g):
        dz, dy = offset(q)
        zz, yy, xx = (z + dz) % Z, (y + dy) % Y, (x + dx) % X
        c = xx * nyz + zz * Y + yy
        pltpu.make_async_remote_copy(
            src_ref=send.at[pl.ds(c * msg, msg)],
            dst_ref=recv.at[pl.ds((q * X + dx) * msg, msg)],
            send_sem=fs, recv_sem=fr.at[g],
            device_id=device(zz, yy, xx, core), device_id_type=MESH,
        ).start()

    own_copy = pltpu.make_async_copy(
        send.at[pl.ds(me * msg, msg)], recv.at[pl.ds(0, msg)], own_sem)
    own_copy.start()
    for dx in range(1, X):
        forward(0, dx, 0)

    def forward_step(q, carry):
        for dx in range(X):
            forward(q, dx, q // GROUP)
        return carry

    lax.fori_loop(1, nyz, forward_step, 0)
    own_copy.wait()

    grows = GROUP * X * msg
    krows = GROUP * X * 2

    def wait_rows(buf, start, count, sem):
        part = buf.at[pl.ds(start, count)]
        pltpu.make_async_copy(part, part, sem).wait()

    def take(buf, g, base, total):
        columns = []
        dead = None
        for t in range(tiles):
            parts = []
            for dx in range(X):
                for s in range(2):
                    start = g * grows + dx * msg + s * tiles + t
                    parts.append(buf[pl.ds(start, GROUP, stride=X * msg), :])
            v = jnp.concatenate(parts, axis=0)
            if dead is None:
                dead = v > 2.0
                bias[pl.ds(base + g * krows, krows), :] = jnp.where(dead, -4.0, 0.0)
            v = jnp.where(dead, 0.0, v)
            hi = v.astype(bf16)
            lo = (v - hi.astype(f32)).astype(bf16)
            khi[pl.ds(base + g * krows, krows), t * 128:(t + 1) * 128] = hi
            klo[pl.ds(base + g * krows, krows), t * 128:(t + 1) * 128] = lo
            columns.append(jnp.sum(v, axis=0, keepdims=True))
        return total + jnp.concatenate(columns, axis=1)

    mine = jnp.zeros((1, width), f32)
    theirs = jnp.zeros((1, width), f32)
    for g in range(n_group):
        missing = msg if g == 0 else 0
        wait_rows(recv, g * grows + missing, grows - missing, fr.at[g])
        pltpu.make_async_remote_copy(
            src_ref=recv.at[pl.ds(g * grows, grows)],
            dst_ref=other.at[pl.ds(g * grows, grows)],
            send_sem=ps, recv_sem=pr.at[g],
            device_id=device(z, y, x, 1 - core), device_id_type=MESH,
        ).start()
        mine = take(recv, g, 0, mine)
        if g > 0:
            wait_rows(other, (g - 1) * grows, grows, pr.at[g - 1])
            theirs = take(other, g - 1, own, theirs)
    wait_rows(other, (n_group - 1) * grows, grows, pr.at[n_group - 1])
    theirs = take(other, n_group - 1, own, theirs)

    sums = mine + theirs
    fresh = sums * lax.rsqrt(jnp.sum(sums * sums, axis=1, keepdims=True) + epsilon)
    for t in range(half_t):
        a = fresh[:, t * 128:(t + 1) * 128]
        b = fresh[:, (half_t + t) * 128:(half_t + t + 1) * 128]
        frow[pl.ds(me * half_t + t, 1), :] = jnp.where(core == 0, a, b)

    def fresh_step(q, carry):
        dz, dy = offset(q)
        part = frow.at[pl.ds(me * half_t, half_t)]
        pltpu.make_async_remote_copy(
            src_ref=part, dst_ref=part, send_sem=ns, recv_sem=nr,
            device_id=device((z + dz) % Z, (y + dy) % Y, x, core), device_id_type=MESH,
        ).start()
        return carry

    lax.fori_loop(1, nyz, fresh_step, 0)

    qh = khi[0:own, :]
    ql = klo[0:own, :]
    block = own // 2

    def sims(kb, best):
        kh = khi[kb * block:(kb + 1) * block, :]
        kl = klo[kb * block:(kb + 1) * block, :]
        s = dot_nt(kh, qh) + dot_nt(kh, ql) + dot_nt(kl, qh)
        off = bias[kb * block:(kb + 1) * block, :]
        s = s + (jnp.concatenate([off] * (own // 128), axis=1) if own > 128 else off[:, :own])
        if kb < 2:
            itself = iota((block, own), 0) + kb * block == iota((block, own), 1)
            s = jnp.where(itself, -4.0, s)
        return jnp.maximum(best, jnp.max(s, axis=0, keepdims=True))

    best = jnp.full((1, own), -1.0, f32)
    best = sims(0, best)
    best = sims(1, best)

    xrows = nyz * half_t
    wait_rows(frow, 0, (nyz - 1) * half_t, nr)

    def pass_on(dx):
        part = pl.ds(((x + X - dx) % X) * xrows, xrows)
        pltpu.make_async_remote_copy(
            src_ref=frow.at[part], dst_ref=fpart.at[part], send_sem=cs, recv_sem=cr.at[dx],
            device_id=device(z, y, x, 1 - core), device_id_type=MESH,
        ).start()

    for dx in range(1, X):
        part = frow.at[pl.ds(x * xrows, xrows)]
        pltpu.make_async_remote_copy(
            src_ref=part, dst_ref=part, send_sem=xs_, recv_sem=xr.at[dx],
            device_id=device(z, y, (x + dx) % X, core), device_id_type=MESH,
        ).start()
    pass_on(0)

    best = sims(2, best)
    best = sims(3, best)

    fh = fresh.astype(bf16)
    fl = jnp.broadcast_to(fresh - fh.astype(f32), (16, width)).astype(bf16)
    fh = jnp.broadcast_to(fresh, (16, width)).astype(bf16)
    cos = (dot_nt(fh, qh) + dot_nt(fh, ql) + dot_nt(fl, qh))[0:1, :]

    lane_of = 2 * ((iota((128, own), 1) // GROUP) % (2 * X))
    j = iota((128, own), 0)
    spread = jnp.where(j == lane_of, best, jnp.where(j == lane_of + 1, cos, 0.0))
    spread = spread.T.reshape(n_group, 2 * X, GROUP, 128)
    abuf[...] = jnp.sum(spread, axis=1).reshape(nyz, 128)
    ans[pl.ds(me, 1), :] = abuf[0:1, :]

    def answer_step(q, carry):
        dz, dy = offset(q)
        pltpu.make_async_remote_copy(
            src_ref=abuf.at[pl.ds(q, 1)], dst_ref=ans.at[pl.ds(me, 1)],
            send_sem=as_, recv_sem=ar,
            device_id=device((z + Z - dz) % Z, (y + Y - dy) % Y, x, core), device_id_type=MESH,
        ).start()
        return carry

    lax.fori_loop(1, nyz, answer_step, 0)

    for dx in range(1, X):
        wait_rows(frow, ((x + X - dx) % X) * xrows, xrows, xr.at[dx])
        pass_on(dx)

    wait_rows(ans, 0, nyz - 1, ar)
    for dx in range(1, X):
        part = ans.at[pl.ds(x * nyz, nyz)]
        pltpu.make_async_remote_copy(
            src_ref=part, dst_ref=part, send_sem=bs, recv_sem=br.at[dx],
            device_id=device(z, y, (x + dx) % X, core), device_id_type=MESH,
        ).start()

    for dx in range(X):
        wait_rows(fpart, ((x + X - dx) % X) * xrows, xrows, cr.at[dx])
    low, high = [], []
    for t in range(half_t):
        a = frow[pl.ds(t, chips, stride=half_t), :]
        b = fpart[pl.ds(t, chips, stride=half_t), :]
        low.append(jnp.where(core == 0, a, b))
        high.append(jnp.where(core == 0, b, a))
    full = jnp.concatenate(low + high, axis=1)
    trows = cent.shape[0]
    row_id = (dp * X + x) * trows + iota((trows, chips), 0)
    hit = jnp.where(row_id == slab[...], 1.0, 0.0)
    named = jnp.sum(hit, axis=1, keepdims=True) > 0.5
    table[...] = jnp.where(named, select_rows(hit.astype(bf16), full), cent[...])

    for dx in range(1, X):
        wait_rows(ans, ((x + X - dx) % X) * nyz, nyz, br.at[dx])
    member = iota((chips, rows), 0) == lrow
    first = member & (rank == 0)
    second = member & (rank == 1)
    got = ans[...]
    dx_of = (iota((chips, 128), 0) // nyz + X - x) % X
    lane = iota((chips, 128), 1) - 4 * dx_of

    def pick(v):
        a = jnp.sum(jnp.where(lane == v, got, 0.0), axis=1, keepdims=True)
        b = jnp.sum(jnp.where(lane == 2 + v, got, 0.0), axis=1, keepdims=True)
        return jnp.sum(jnp.where(first, a, jnp.where(second, b, 0.0)), axis=0, keepdims=True)

    sim_out[...] = pick(0)
    cos_out[...] = pick(1)

    wait_rows(send, 0, (chips - 1) * msg, fs)
    wait_rows(recv, 0, n_group * grows, ps)
    wait_rows(frow, 0, (nyz - 1) * half_t, ns)
    wait_rows(frow, 0, (X - 1) * xrows, xs_)
    wait_rows(frow, 0, X * xrows, cs)
    wait_rows(ans, 0, nyz - 1, as_)
    wait_rows(ans, 0, (X - 1) * nyz, bs)


def local(dims, embeddings, assignment, slab_ids, centroids):
    Z, Y, X = dims
    nyz = Z * Y
    chips = nyz * X
    rows, width = embeddings.shape
    tiles = width // 128
    n_group = nyz // GROUP
    linear = 2 * chips * tiles
    dma = pltpu.SemaphoreType.DMA
    vmem = pl.BlockSpec(memory_space=pltpu.VMEM)
    table, cos, sim = pl.pallas_call(
        functools.partial(kernel, dims),
        out_shape=(
            jax.ShapeDtypeStruct(centroids.shape, f32),
            jax.ShapeDtypeStruct((1, rows), f32),
            jax.ShapeDtypeStruct((1, rows), f32),
        ),
        in_specs=[vmem] * 4,
        out_specs=(vmem,) * 3,
        scratch_shapes=[
            pltpu.VMEM((linear, 128), f32),
            pltpu.VMEM((linear, 128), f32),
            pltpu.VMEM((linear, 128), f32),
            pltpu.VMEM((4 * chips, width), bf16),
            pltpu.VMEM((4 * chips, width), bf16),
            pltpu.VMEM((4 * chips, 128), f32),
            pltpu.VMEM((chips * tiles // 2, 128), f32),
            pltpu.VMEM((chips * tiles // 2, 128), f32),
            pltpu.VMEM((nyz, 128), f32),
            pltpu.VMEM((chips, 128), f32),
            pltpu.SemaphoreType.REGULAR,
            pltpu.SemaphoreType.REGULAR,
            dma,
            dma, dma((n_group,)), dma, dma((n_group,)),
            dma, dma, dma, dma((X,)), dma, dma((X,)),
            dma, dma, dma, dma((X,)),
        ],
        compiler_params=pltpu.CompilerParams(
            collective_id=0, has_side_effects=True, vmem_limit_bytes=40 * 2**20
        ),
    )(embeddings, assignment.reshape(1, rows), slab_ids.reshape(1, chips), centroids)
    return table, cos.reshape(rows), sim.reshape(rows)


def solution(mesh, dims=(Z, Y, X)):
    placed = (P(("dp", "cent"), None), P(("dp", "cent"), None), P(), P(("dp", "cent"), None))
    return jax.shard_map(
        functools.partial(local, dims),
        mesh=mesh,
        in_specs=placed,
        out_specs=(P(("dp", "cent"), None), P(("dp", "cent")), P(("dp", "cent"))),
        check_vma=False,
    )
```

```python
import functools

import jax
import jax.numpy as jnp
from jax import lax
from jax.experimental import pallas as pl
from jax.experimental.pallas import tpu as pltpu
from jax.sharding import PartitionSpec as P

epsilon = 1e-06
Z, Y, X = 8, 8, 4
GROUP = 8
SENTINEL = 4.0
MESH = pl.DeviceIdType.MESH
f32, bf16 = jnp.float32, jnp.bfloat16


def split3(v):
    hi = v.astype(bf16)
    rest = v - hi.astype(f32)
    mid = rest.astype(bf16)
    lo = (rest - mid.astype(f32)).astype(bf16)
    return hi, mid, lo


def select_rows(onehot, v):
    hi, mid, lo = split3(v)
    dot = functools.partial(jnp.dot, preferred_element_type=f32)
    return dot(onehot, hi) + dot(onehot, mid) + dot(onehot, lo)


def dot_nt(a, b):
    return lax.dot_general(a, b, (((1,), (1,)), ((), ())), preferred_element_type=f32)


def yz_offsets(Z, Y):
    seen, runs = {(0, 0)}, []
    for dz in range(Z):
        for dy in range(Y):
            run, a, b = [], dz, dy
            for _ in range(4):
                if (a, b) not in seen:
                    seen.add((a, b))
                    run.append((a, b))
                if Z == Y:
                    a, b = -b % Z, a
            if run:
                runs.append(run)

    def far(run):
        a, b = run[0]
        return -(min(a, Z - a) + min(b, Y - b))

    return [(0, 0)] + [o for run in sorted(runs, key=far) for o in run]


def iota(shape, axis):
    return lax.broadcasted_iota(jnp.int32, shape, axis)


def kernel(dims, emb_hbm, lab_hbm, slab_hbm, cent_hbm, table, cos_out, sim_out,
           emb, lab, slab, cent,
           send, stage, out, recv, other, khi, klo, bias, frow, fpart, abuf, ans,
           line_sem, load, gs, gr,
           fs, fr, ps, pr, ns, nr, xs_, xr, cs, cr, as_, ar, bs, br):
    Z, Y, X = dims
    nyz = Z * Y
    chips = nyz * X
    n_group = nyz // GROUP
    rows, width = emb.shape
    tiles = width // 128
    half_t = tiles // 2
    msg = 2 * tiles
    own = 2 * chips
    offsets = yz_offsets(Z, Y)

    loads = [
        pltpu.make_async_copy(src, dst, load.at[i])
        for i, (src, dst) in enumerate(
            ((emb_hbm, emb), (lab_hbm, lab), (slab_hbm, slab), (cent_hbm, cent)))
    ]
    for copy in loads:
        copy.start()

    dp = lax.axis_index("dp")
    x = lax.axis_index("cent")
    core = dp % 2
    yz = dp // 2
    y = yz % Y
    z = yz // Y
    me = x * nyz + yz

    def device(zz, yy, xx, cc):
        return ((zz * Y + yy) * 2 + cc, xx)

    barrier = pltpu.get_barrier_semaphore()

    def signal(sem, zz, yy, xx, cc):
        pl.semaphore_signal(sem, inc=1, device_id=device(zz, yy, xx, cc), device_id_type=MESH)

    for d in range(1, Z):
        signal(barrier, (z + d) % Z, y, x, core)
    for d in range(1, Y):
        signal(barrier, z, (y + d) % Y, x, core)
    for d in range(1, X):
        signal(barrier, z, y, (x + d) % X, core)
    signal(barrier, z, y, x, 1 - core)

    loads[0].wait()
    loads[1].wait()
    e = emb[...]
    unit = e * lax.rsqrt(jnp.sum(e * e, axis=1, keepdims=True) + epsilon)

    pl.semaphore_wait(barrier, Z + Y + X - 2)
    for d in range(1, Y):
        signal(line_sem, z, (y + d) % Y, x, core)

    lrow = lab[...]
    lcol = jnp.broadcast_to(lrow.astype(f32), (128, rows)).T[:, 0:1].astype(jnp.int32)
    earlier = (lcol == lrow) & (iota((rows, rows), 0) < iota((rows, rows), 1))
    rank = jnp.sum(jnp.where(earlier, 1.0, 0.0), axis=0, keepdims=True).astype(jnp.int32)
    lx, lyz = lrow // nyz, lrow % nyz
    dx_row = (lx + X - x) % X
    code = ((lyz // Y + Z - z) % Z) * Y + (lyz % Y + Y - y) % Y
    q_row = jnp.zeros((1, rows), jnp.int32)
    for q, (dz, dy) in enumerate(offsets):
        q_row = jnp.where(code == dz * Y + dy, q, q_row)
    target = 2 * (((q_row // GROUP) * X + dx_row) * GROUP + q_row % GROUP) + rank
    place = jnp.where(iota((own, rows), 0) == target, 1.0, 0.0)
    filled = jnp.sum(place, axis=1, keepdims=True) > 0.5
    slots = select_rows(place.astype(bf16), unit)
    slots = jnp.where(filled, slots, SENTINEL)
    for t in range(tiles):
        send[pl.ds(t, own, stride=tiles), :] = slots[:, t * 128:(t + 1) * 128]

    block_rows = GROUP * msg
    for g in range(n_group):
        for dx in range(1, X):
            pltpu.make_async_remote_copy(
                src_ref=send.at[pl.ds((g * X + dx) * block_rows, block_rows)],
                dst_ref=stage.at[pl.ds((g * (X - 1) + dx - 1) * block_rows, block_rows)],
                send_sem=gs, recv_sem=gr.at[g],
                device_id=device(z, y, (x + dx) % X, core), device_id_type=MESH,
            ).start()

    pl.semaphore_wait(line_sem, Y - 1)

    def wait_rows(buf, start, count, sem):
        part = buf.at[pl.ds(start, count)]
        pltpu.make_async_copy(part, part, sem).wait()

    zs = [(z + d) % Z for d in range(Z)]
    ys = [(y + d) % Y for d in range(Y)]

    def away(q):
        dz, dy = offsets[q]
        return device(zs[dz], ys[dy], x, core)

    def back(q):
        dz, dy = offsets[q]
        return device(zs[-dz % Z], ys[-dy % Y], x, core)

    for g in range(n_group):
        wait_rows(stage, g * (X - 1) * block_rows, (X - 1) * block_rows, gr.at[g])
        for j in range(GROUP):
            q = g * GROUP + j
            into = recv if q == 0 else out
            for dx in range(X):
                if dx == 0:
                    piece = send[pl.ds(g * X * block_rows + j * msg, msg), :]
                else:
                    piece = stage[pl.ds((g * (X - 1) + dx - 1) * block_rows + j * msg, msg), :]
                into[pl.ds((q * X + dx) * msg, msg), :] = piece
        for j in range(GROUP):
            q = g * GROUP + j
            if q > 0:
                pltpu.make_async_remote_copy(
                    src_ref=out.at[pl.ds(q * X * msg, X * msg)],
                    dst_ref=recv.at[pl.ds(q * X * msg, X * msg)],
                    send_sem=fs, recv_sem=fr.at[g],
                    device_id=away(q), device_id_type=MESH,
                ).start()

    grows = GROUP * X * msg
    krows = GROUP * X * 2

    def take(buf, g, base, total):
        columns = []
        dead = None
        for t in range(tiles):
            parts = []
            for dx in range(X):
                for s in range(2):
                    start = g * grows + dx * msg + s * tiles + t
                    parts.append(buf[pl.ds(start, GROUP, stride=X * msg), :])
            v = jnp.concatenate(parts, axis=0)
            if dead is None:
                dead = v > 2.0
                bias[pl.ds(base + g * krows, krows), :] = jnp.where(dead, -4.0, 0.0)
            v = jnp.where(dead, 0.0, v)
            hi = v.astype(bf16)
            lo = (v - hi.astype(f32)).astype(bf16)
            khi[pl.ds(base + g * krows, krows), t * 128:(t + 1) * 128] = hi
            klo[pl.ds(base + g * krows, krows), t * 128:(t + 1) * 128] = lo
            columns.append(jnp.sum(v, axis=0, keepdims=True))
        return total + jnp.concatenate(columns, axis=1)

    mine = jnp.zeros((1, width), f32)
    theirs = jnp.zeros((1, width), f32)
    for g in range(n_group):
        missing = X * msg if g == 0 else 0
        wait_rows(recv, g * grows + missing, grows - missing, fr.at[g])
        pltpu.make_async_remote_copy(
            src_ref=recv.at[pl.ds(g * grows, grows)],
            dst_ref=other.at[pl.ds(g * grows, grows)],
            send_sem=ps, recv_sem=pr.at[g],
            device_id=device(z, y, x, 1 - core), device_id_type=MESH,
        ).start()
        mine = take(recv, g, 0, mine)
        if g > 0:
            wait_rows(other, (g - 1) * grows, grows, pr.at[g - 1])
            theirs = take(other, g - 1, own, theirs)
    wait_rows(other, (n_group - 1) * grows, grows, pr.at[n_group - 1])
    theirs = take(other, n_group - 1, own, theirs)

    sums = mine + theirs
    fresh = sums * lax.rsqrt(jnp.sum(sums * sums, axis=1, keepdims=True) + epsilon)
    for t in range(half_t):
        a = fresh[:, t * 128:(t + 1) * 128]
        b = fresh[:, (half_t + t) * 128:(half_t + t + 1) * 128]
        frow[pl.ds(me * half_t + t, 1), :] = jnp.where(core == 0, a, b)

    for q in range(1, nyz):
        part = frow.at[pl.ds(me * half_t, half_t)]
        pltpu.make_async_remote_copy(
            src_ref=part, dst_ref=part, send_sem=ns, recv_sem=nr,
            device_id=away(q), device_id_type=MESH,
        ).start()

    qh = khi[0:own, :]
    ql = klo[0:own, :]
    block = own // 2

    def sims(kb, best):
        kh = khi[kb * block:(kb + 1) * block, :]
        kl = klo[kb * block:(kb + 1) * block, :]
        s = dot_nt(kh, qh) + dot_nt(kh, ql) + dot_nt(kl, qh)
        off = bias[kb * block:(kb + 1) * block, :]
        s = s + (jnp.concatenate([off] * (own // 128), axis=1) if own > 128 else off[:, :own])
        if kb < 2:
            itself = iota((block, own), 0) + kb * block == iota((block, own), 1)
            s = jnp.where(itself, -4.0, s)
        return jnp.maximum(best, jnp.max(s, axis=0, keepdims=True))

    best = jnp.full((1, own), -1.0, f32)
    best = sims(0, best)
    best = sims(1, best)

    xrows = nyz * half_t
    wait_rows(frow, 0, (nyz - 1) * half_t, nr)

    def pass_on(dx):
        part = pl.ds(((x + X - dx) % X) * xrows, xrows)
        pltpu.make_async_remote_copy(
            src_ref=frow.at[part], dst_ref=fpart.at[part], send_sem=cs, recv_sem=cr.at[dx],
            device_id=device(z, y, x, 1 - core), device_id_type=MESH,
        ).start()

    for dx in range(1, X):
        part = frow.at[pl.ds(x * xrows, xrows)]
        pltpu.make_async_remote_copy(
            src_ref=part, dst_ref=part, send_sem=xs_, recv_sem=xr.at[dx],
            device_id=device(z, y, (x + dx) % X, core), device_id_type=MESH,
        ).start()
    pass_on(0)

    best = sims(2, best)
    best = sims(3, best)

    fh = fresh.astype(bf16)
    fl = jnp.broadcast_to(fresh - fh.astype(f32), (16, width)).astype(bf16)
    fh = jnp.broadcast_to(fresh, (16, width)).astype(bf16)
    cos = (dot_nt(fh, qh) + dot_nt(fh, ql) + dot_nt(fl, qh))[0:1, :]

    lane_of = 2 * ((iota((128, own), 1) // GROUP) % (2 * X))
    j = iota((128, own), 0)
    spread = jnp.where(j == lane_of, best, jnp.where(j == lane_of + 1, cos, 0.0))
    spread = spread.T.reshape(n_group, 2 * X, GROUP, 128)
    abuf[...] = jnp.sum(spread, axis=1).reshape(nyz, 128)
    ans[pl.ds(me, 1), :] = abuf[0:1, :]

    for q in range(1, nyz):
        pltpu.make_async_remote_copy(
            src_ref=abuf.at[pl.ds(q, 1)], dst_ref=ans.at[pl.ds(me, 1)],
            send_sem=as_, recv_sem=ar,
            device_id=back(q), device_id_type=MESH,
        ).start()

    for dx in range(1, X):
        wait_rows(frow, ((x + X - dx) % X) * xrows, xrows, xr.at[dx])
        pass_on(dx)

    wait_rows(ans, 0, nyz - 1, ar)
    for dx in range(1, X):
        part = ans.at[pl.ds(x * nyz, nyz)]
        pltpu.make_async_remote_copy(
            src_ref=part, dst_ref=part, send_sem=bs, recv_sem=br.at[dx],
            device_id=device(z, y, (x + dx) % X, core), device_id_type=MESH,
        ).start()

    loads[2].wait()
    loads[3].wait()
    for dx in range(X):
        wait_rows(fpart, ((x + X - dx) % X) * xrows, xrows, cr.at[dx])
    low, high = [], []
    for t in range(half_t):
        a = frow[pl.ds(t, chips, stride=half_t), :]
        b = fpart[pl.ds(t, chips, stride=half_t), :]
        low.append(jnp.where(core == 0, a, b))
        high.append(jnp.where(core == 0, b, a))
    full = jnp.concatenate(low + high, axis=1)
    trows = cent.shape[0]
    row_id = (dp * X + x) * trows + iota((trows, chips), 0)
    hit = jnp.where(row_id == slab[...], 1.0, 0.0)
    named = jnp.sum(hit, axis=1, keepdims=True) > 0.5
    table[...] = jnp.where(named, select_rows(hit.astype(bf16), full), cent[...])

    for dx in range(1, X):
        wait_rows(ans, ((x + X - dx) % X) * nyz, nyz, br.at[dx])
    member = iota((chips, rows), 0) == lrow
    first = member & (rank == 0)
    second = member & (rank == 1)
    got = ans[...]
    dx_of = (iota((chips, 128), 0) // nyz + X - x) % X
    lane = iota((chips, 128), 1) - 4 * dx_of

    def pick(v):
        a = jnp.sum(jnp.where(lane == v, got, 0.0), axis=1, keepdims=True)
        b = jnp.sum(jnp.where(lane == 2 + v, got, 0.0), axis=1, keepdims=True)
        return jnp.sum(jnp.where(first, a, jnp.where(second, b, 0.0)), axis=0, keepdims=True)

    sim_out[...] = pick(0)
    cos_out[...] = pick(1)

    wait_rows(send, 0, n_group * (X - 1) * block_rows, gs)
    wait_rows(out, 0, (nyz - 1) * X * msg, fs)
    wait_rows(recv, 0, n_group * grows, ps)
    wait_rows(frow, 0, (nyz - 1) * half_t, ns)
    wait_rows(frow, 0, (X - 1) * xrows, xs_)
    wait_rows(frow, 0, X * xrows, cs)
    wait_rows(ans, 0, nyz - 1, as_)
    wait_rows(ans, 0, (X - 1) * nyz, bs)


def store(table, cos, sim, table_out, cos_out, sim_out, sems):
    copies = [
        pltpu.make_async_copy(src, dst, sems.at[i])
        for i, (src, dst) in enumerate(((table, table_out), (cos, cos_out), (sim, sim_out)))
    ]
    for copy in copies:
        copy.start()
    for copy in copies:
        copy.wait()


def local(dims, embeddings, assignment, slab_ids, centroids):
    Z, Y, X = dims
    nyz = Z * Y
    chips = nyz * X
    rows, width = embeddings.shape
    tiles = width // 128
    n_group = nyz // GROUP
    linear = 2 * chips * tiles
    dma = pltpu.SemaphoreType.DMA
    vmem = pl.BlockSpec(memory_space=pltpu.VMEM)
    hbm = pl.BlockSpec(memory_space=pl.ANY)
    outs = (
        jax.ShapeDtypeStruct(centroids.shape, f32),
        jax.ShapeDtypeStruct((1, rows), f32),
        jax.ShapeDtypeStruct((1, rows), f32),
    )
    results = pl.pallas_call(
        functools.partial(kernel, dims),
        out_shape=outs,
        in_specs=[pl.BlockSpec(memory_space=pltpu.HBM)] * 4,
        out_specs=(vmem,) * 3,
        scratch_shapes=[
            pltpu.VMEM((rows, width), f32),
            pltpu.VMEM((1, rows), jnp.int32),
            pltpu.VMEM((1, chips), jnp.int32),
            pltpu.VMEM(centroids.shape, f32),
            pltpu.VMEM((linear, 128), f32),
            pltpu.VMEM((linear // X * (X - 1), 128), f32),
            pltpu.VMEM((linear, 128), f32),
            pltpu.VMEM((linear, 128), f32),
            pltpu.VMEM((linear, 128), f32),
            pltpu.VMEM((4 * chips, width), bf16),
            pltpu.VMEM((4 * chips, width), bf16),
            pltpu.VMEM((4 * chips, 128), f32),
            pltpu.VMEM((chips * tiles // 2, 128), f32),
            pltpu.VMEM((chips * tiles // 2, 128), f32),
            pltpu.VMEM((nyz, 128), f32),
            pltpu.VMEM((chips, 128), f32),
            pltpu.SemaphoreType.REGULAR,
            dma((4,)), dma, dma((n_group,)),
            dma, dma((n_group,)), dma, dma((n_group,)),
            dma, dma, dma, dma((X,)), dma, dma((X,)),
            dma, dma, dma, dma((X,)),
        ],
        compiler_params=pltpu.CompilerParams(
            collective_id=0, has_side_effects=True, vmem_limit_bytes=107 * 2**19
        ),
    )(embeddings, assignment.reshape(1, rows), slab_ids.reshape(1, chips), centroids)
    table, cos, sim = pl.pallas_call(
        store,
        out_shape=outs,
        in_specs=[vmem] * 3,
        out_specs=(hbm,) * 3,
        scratch_shapes=[dma((3,))],
    )(*results)
    return table, cos.reshape(rows), sim.reshape(rows)


def solution(mesh, dims=(Z, Y, X)):
    placed = (P(("dp", "cent"), None), P(("dp", "cent"), None), P(), P(("dp", "cent"), None))
    return jax.shard_map(
        functools.partial(local, dims),
        mesh=mesh,
        in_specs=placed,
        out_specs=(P(("dp", "cent"), None), P(("dp", "cent")), P(("dp", "cent"))),
        check_vma=False,
    )
```

```python
import functools

import jax
import jax.numpy as jnp
from jax import lax
from jax.experimental import pallas as pl
from jax.experimental.pallas import tpu as pltpu
from jax.sharding import PartitionSpec as P

epsilon = 1e-06
Z, Y, X = 8, 8, 4
GROUP = 8
KERNEL_BYTES = 105 * 2**19
SENTINEL = 4.0
MESH = pl.DeviceIdType.MESH
f32, bf16 = jnp.float32, jnp.bfloat16


def split3(v):
    hi = v.astype(bf16)
    rest = v - hi.astype(f32)
    mid = rest.astype(bf16)
    lo = (rest - mid.astype(f32)).astype(bf16)
    return hi, mid, lo


def select_rows(onehot, v):
    hi, mid, lo = split3(v)
    dot = functools.partial(jnp.dot, preferred_element_type=f32)
    return dot(onehot, hi) + dot(onehot, mid) + dot(onehot, lo)


def plan(Z, Y):
    def step(d, other, n):
        return 0 if 2 * d != n else (1 if other % 2 == 0 else -1)

    ties = {}
    for dz in range(Z):
        for dy in range(Y):
            shift = (step(dz, dy, Z), step(dy, dz, Y))
            if shift != (0, 0):
                ties.setdefault(shift, []).append((dz, dy))
    offsets, batches = [(0, 0)], []
    for shift in ((1, 1), (1, 0), (0, 1), (-1, 0), (0, -1)):
        batches.append((len(offsets), len(ties[shift])) + shift)
        offsets += ties[shift]
    seen, runs = set(offsets), []
    for dz in range(Z):
        for dy in range(Y):
            run, a, b = [], dz, dy
            for _ in range(4):
                if (a, b) not in seen:
                    seen.add((a, b))
                    run.append((a, b))
                a, b = -b % Z, a
            if run:
                runs.append(run)
    runs.sort(key=lambda run: -sum(min(d, Z - d) for d in run[0]))
    rest = [o for run in runs for o in run]
    return offsets + rest, batches


def iota(shape, axis):
    return lax.broadcasted_iota(jnp.int32, shape, axis)


def position():
    dp = lax.axis_index("dp")
    return dp, lax.axis_index("cent"), dp % 2


def wait_rows(buf, start, count, sem):
    part = buf.at[pl.ds(start, count)]
    pltpu.make_async_copy(part, part, sem).wait()


def ranks(lrow):
    rows = lrow.shape[1]
    lcol = jnp.broadcast_to(lrow.astype(f32), (128, rows)).T[:, 0:1].astype(jnp.int32)
    earlier = (lcol == lrow) & (iota((rows, rows), 0) < iota((rows, rows), 1))
    return jnp.sum(jnp.where(earlier, 1.0, 0.0), axis=0, keepdims=True).astype(jnp.int32)


def exchange(dims, emb_hbm, lab_hbm, frow, fpart, ans,
             emb, lab, send, stage, out, recv, other, khi, klo, qht, qlt, bias,
             abuf, ay, ab, az,
             line_sem, plane_sem, load, gs, gr, fs, fr, ps, pr,
             nys, nyr, nzs, nzr, nxs, nxr, ncs, ncr, ays, ayr, azs, azr, axs, axr):
    Z, Y, X = dims
    nyz = Z * Y
    chips = nyz * X
    n_group = nyz // GROUP
    rows, width = emb.shape
    tiles = width // 128
    half_t = tiles // 2
    msg = 2 * tiles
    own = 2 * chips
    offsets, batches = plan(Z, Y)
    tied = sum(n for _, n, _, _ in batches) + 1

    loads = [pltpu.make_async_copy(lab_hbm, lab, load.at[0])]
    part = rows // 4
    loads += [
        pltpu.make_async_copy(
            emb_hbm.at[pl.ds(i * part, part)], emb.at[pl.ds(i * part, part)], load.at[1 + i])
        for i in range(4)
    ]
    for copy in loads:
        copy.start()

    dp, x, core = position()
    yz = dp // 2
    y = yz % Y
    z = yz // Y
    me = x * nyz + yz
    zs = [(z + d) % Z for d in range(Z)]
    ys = [(y + d) % Y for d in range(Y)]
    partner = (yz * 2 + 1 - core, x)

    def at(dz, dy, dx=0):
        return ((zs[dz % Z] * Y + ys[dy % Y]) * 2 + core, (x + dx) % X)

    def signal(sem, where):
        pl.semaphore_signal(sem, inc=1, device_id=where, device_id_type=MESH)

    def start(src, dst, send_sem, recv_sem, where):
        pltpu.make_async_remote_copy(
            src_ref=src, dst_ref=dst, send_sem=send_sem, recv_sem=recv_sem,
            device_id=where, device_id_type=MESH,
        ).start()

    barrier = pltpu.get_barrier_semaphore()
    for d in range(1, Z):
        signal(barrier, at(d, 0))
    for d in range(1, Y):
        signal(barrier, at(0, d))
    for d in range(1, X):
        signal(barrier, at(0, 0, d))
    signal(barrier, partner)

    loads[0].wait()
    lrow = lab[...]
    rank = ranks(lrow)
    lx, lyz = lrow // nyz, lrow % nyz
    dx_row = (lx + X - x) % X
    code = ((lyz // Y + Z - z) % Z) * Y + (lyz % Y + Y - y) % Y
    first_slot = jnp.zeros((1, rows), jnp.int32)
    per_dx = jnp.ones((1, rows), jnp.int32)
    for q, (dz, dy) in enumerate(offsets):
        if q == 0 or q >= tied:
            first_slot = jnp.where(code == dz * Y + dy, q * X, first_slot)
    for q0, n, _, _ in batches:
        for q in range(q0, q0 + n):
            here = code == offsets[q][0] * Y + offsets[q][1]
            first_slot = jnp.where(here, q0 * X + q - q0, first_slot)
            per_dx = jnp.where(here, n, per_dx)
    target = 2 * (first_slot + dx_row * per_dx) + rank

    pl.semaphore_wait(barrier, Z + Y + X - 2)
    for d in range(1, Y):
        signal(line_sem, at(0, d))

    for copy in loads[1:]:
        copy.wait()
    e = emb[...]
    unit = e * lax.rsqrt(jnp.sum(e * e, axis=1, keepdims=True) + epsilon)
    parts = split3(unit)

    n_chunk = min(4, n_group)
    chunk = own // n_chunk
    chunk_q = nyz // n_chunk

    def fill(i):
        low = i * chunk
        place = jnp.where(iota((chunk, rows), 0) + low == target, 1.0, 0.0)
        filled = jnp.sum(place, axis=1, keepdims=True) > 0.5
        place = place.astype(bf16)
        slots = sum(jnp.dot(place, p, preferred_element_type=f32) for p in parts)
        slots = jnp.where(filled, slots, SENTINEL)
        for t in range(tiles):
            send[pl.ds(low * tiles + t, chunk, stride=tiles), :] = (
                slots[:, t * 128:(t + 1) * 128])

    def straight(q, dx):
        piece = pl.ds((q * X + dx) * msg, msg)
        start(send.at[piece], recv.at[piece], fs, fr.at[q // GROUP], at(*offsets[q], dx))

    def straight_all(i):
        def step(dx, carry):
            for q in range(i * chunk_q, (i + 1) * chunk_q):
                straight(q, dx)
            return carry
        lax.fori_loop(1, X, step, 0)

    fill(1)
    pl.semaphore_wait(line_sem, Y - 1)
    for d in range(1, X):
        signal(plane_sem, at(0, 0, d))
    for q in range(chunk_q, 2 * chunk_q):
        straight(q, 0)
    fill(0)
    pl.semaphore_wait(plane_sem, X - 1)
    for b, (q0, n, sz, sy) in enumerate(batches):
        for dx in range(X):
            piece = pl.ds((q0 * X + dx * n) * msg, n * msg)
            start(send.at[piece], stage.at[piece], gs, gr.at[b], at(sz, sy, dx))
    for dx in range(1, X):
        straight(0, dx)
    recv[0:msg, :] = send[0:msg, :]
    straight_all(1)
    for b, (q0, n, sz, sy) in enumerate(batches):
        wait_rows(stage, q0 * X * msg, X * n * msg, gr.at[b])
        for q in range(q0, q0 + n):
            for dx in range(X):
                piece = stage[pl.ds((q0 * X + dx * n + q - q0) * msg, msg), :]
                out[pl.ds((q * X + dx) * msg, msg), :] = piece
        for q in range(q0, q0 + n):
            piece = pl.ds(q * X * msg, X * msg)
            start(out.at[piece], recv.at[piece], fs, fr.at[q // GROUP],
                  at(offsets[q][0] - sz, offsets[q][1] - sy))
    for i in range(2, n_chunk):
        fill(i)
        for q in range(i * chunk_q, (i + 1) * chunk_q):
            straight(q, 0)
        straight_all(i)

    grows = GROUP * X * msg
    krows = GROUP * X * 2

    def take(buf, g, base, total):
        columns = []
        dead = None
        for t in range(tiles):
            pieces = []
            for dx in range(X):
                for s in range(2):
                    first = g * grows + dx * msg + s * tiles + t
                    pieces.append(buf[pl.ds(first, GROUP, stride=X * msg), :])
            v = jnp.concatenate(pieces, axis=0)
            if dead is None:
                dead = v > 2.0
                bias[pl.ds(base + g * krows, krows), :] = jnp.where(dead, -4.0, 0.0)
            v = jnp.where(dead, 0.0, v)
            hi = v.astype(bf16)
            lo = (v - hi.astype(f32)).astype(bf16)
            khi[pl.ds(base + g * krows, krows), t * 128:(t + 1) * 128] = hi
            klo[pl.ds(base + g * krows, krows), t * 128:(t + 1) * 128] = lo
            columns.append(jnp.sum(v, axis=0, keepdims=True))
        return total + jnp.concatenate(columns, axis=1)

    mine = jnp.zeros((1, width), f32)
    theirs = jnp.zeros((1, width), f32)
    per_chunk = n_group // n_chunk
    order = [g for i in [1, 0] + list(range(2, n_chunk))
             for g in range(i * per_chunk, (i + 1) * per_chunk)]
    done = set()
    for g in order:
        missing = msg if g == 0 else 0
        wait_rows(recv, g * grows + missing, grows - missing, fr.at[g])
        piece = pl.ds(g * grows, grows)
        start(recv.at[piece], other.at[piece], ps, pr.at[g], partner)
        mine = take(recv, g, 0, mine)
        done.add(g)
        block = g * krows // 128
        members = [h for h in range(n_group) if h * krows // 128 == block]
        if done.issuperset(members):
            top = pl.ds(block * 128, min(128, own))
            for t in range(tiles):
                lanes = pl.ds(t * 128, 128)
                qht[lanes, top] = khi[top, lanes].astype(f32).T.astype(bf16)
                qlt[lanes, top] = klo[top, lanes].astype(f32).T.astype(bf16)
        wait_rows(other, g * grows, grows, pr.at[g])
        theirs = take(other, g, own, theirs)

    sums = mine + theirs
    fresh = sums * lax.rsqrt(jnp.sum(sums * sums, axis=1, keepdims=True) + epsilon)
    for t in range(half_t):
        a = fresh[:, t * 128:(t + 1) * 128]
        b = fresh[:, (half_t + t) * 128:(half_t + t + 1) * 128]
        frow[pl.ds(me * half_t + t, 1), :] = jnp.where(core == 0, a, b)
    piece = pl.ds(me * half_t, half_t)
    for d in range(1, Y):
        start(frow.at[piece], frow.at[piece], nys, nyr, at(0, d))
    fh = fresh.astype(bf16)
    khi[2 * own:2 * own + 16, :] = jnp.broadcast_to(fresh, (16, width)).astype(bf16)
    klo[2 * own:2 * own + 16, :] = jnp.broadcast_to(
        fresh - fh.astype(f32), (16, width)).astype(bf16)

    def product(first, count):
        kh = khi[first:first + count, :]
        kl = klo[first:first + count, :]
        dot = functools.partial(jnp.dot, preferred_element_type=f32)
        return dot(kh, qht[...]) + dot(kh, qlt[...]) + dot(kl, qht[...])

    def closest(s, first):
        off = bias[first:first + own, :]
        s = s + (jnp.concatenate([off] * (own // 128), axis=1) if own > 128 else off[:, :own])
        if first == 0:
            s = jnp.where(iota((own, own), 0) == iota((own, own), 1), -4.0, s)
        return jnp.max(s, axis=0, keepdims=True)

    best = jnp.maximum(closest(product(0, own), 0), -1.0)

    yrows = Y * half_t
    wait_rows(frow, 0, (Y - 1) * half_t, nyr)
    piece = pl.ds((x * nyz + z * Y) * half_t, yrows)
    for d in range(1, Z):
        start(frow.at[piece], frow.at[piece], nzs, nzr, at(d, 0))

    s = product(own, own + 16)
    best = jnp.maximum(best, closest(s[:own, :], own))
    cos = s[own:own + 1, :]

    xs = (iota((128, own), 1) // GROUP) % (2 * X)
    lane_of = (xs // 2) * 8 + (xs % 2) * 2
    j = iota((128, own), 0)
    spread = jnp.where(j == lane_of, best, jnp.where(j == lane_of + 1, cos, 0.0))
    spread = spread.T.reshape(n_group, 2 * X, GROUP, 128)
    spread = jnp.sum(spread, axis=1).reshape(nyz, 128)
    for q, (dz, dy) in enumerate(offsets):
        abuf[dy * Z + dz:dy * Z + dz + 1, :] = spread[q:q + 1, :]
    for d in range(1, Y):
        start(abuf.at[pl.ds(d * Z, Z)], ay.at[pl.ds(y * Z, Z)], ays, ayr, at(0, -d))
    ay[pl.ds(y * Z, Z), :] = abuf[0:Z, :]

    xrows = nyz * half_t
    hrows = xrows // 2

    def block_of(dx, half):
        return pl.ds(((x + dx) % X) * xrows + half * hrows, hrows)

    def along(dx, half, sem, to):
        piece = block_of(dx, half)
        start(frow.at[piece], frow.at[piece], nxs, nxr.at[sem], at(0, 0, to))

    def pass_on(dx):
        piece = pl.ds(((x + dx) % X) * xrows, xrows)
        start(frow.at[piece], fpart.at[piece], ncs, ncr.at[dx], partner)

    def landed(dx, half, sem):
        wait_rows(frow, ((x + dx) % X) * xrows + half * hrows, hrows, nxr.at[sem])

    wait_rows(frow, 0, (Z - 1) * yrows, nzr)
    along(0, 0, 0, 1)
    if X > 2:
        along(0, 1, 2, X - 1)
    along(0, 1, 1, 1)
    if X > 2:
        along(0, 0, 3, X - 1)
    pass_on(0)
    if X > 2:
        landed(X - 1, 0, 0)
        along(X - 1, 0, 4, 1)
        landed(1, 1, 2)
        along(1, 1, 5, X - 1)

    wait_rows(ay, 0, (Y - 1) * Z, ayr)
    for dz in range(Z):
        ab[dz * Y:(dz + 1) * Y, :] = ay[pl.ds(dz, Y, stride=Z), :]
    for d in range(1, Z):
        start(ab.at[pl.ds(d * Y, Y)], az.at[pl.ds(z * Y, Y)], azs, azr, at(-d, 0))
    az[pl.ds(z * Y, Y), :] = ab[0:Y, :]

    if X > 2:
        landed(X - 1, 1, 1)
        pass_on(X - 1)
        landed(1, 0, 3)
        pass_on(1)
    else:
        landed(1, 0, 0)
        landed(1, 1, 1)
        pass_on(1)

    wait_rows(az, 0, (Z - 1) * Y, azr)
    wait_rows(ay, 0, (Y - 1) * Z, ays)
    turned = jnp.concatenate([az[...], jnp.zeros((128 - nyz, 128), f32)], axis=0).T
    abuf[0:8 * X, :] = turned[0:8 * X, :]
    for d in range(1, X):
        start(abuf.at[pl.ds(d * 8, 8)], ans.at[pl.ds(x * 8, 8)], axs, axr, at(0, 0, X - d))
    ans[pl.ds(x * 8, 8), :] = abuf[0:8, :]

    if X > 2:
        landed(2, 0, 4)
        landed(2, 1, 5)
        pass_on(2)
    for dx in range(X):
        wait_rows(fpart, ((x + dx) % X) * xrows, xrows, ncr.at[dx])
    wait_rows(ans, 0, (X - 1) * 8, axr)

    wait_rows(send, 0, (tied - 1) * X * msg, gs)
    wait_rows(send, 0, (chips - 1) * msg, fs)
    wait_rows(recv, 0, n_group * grows, ps)
    wait_rows(frow, 0, (Y - 1) * half_t, nys)
    wait_rows(frow, 0, (Z - 1) * yrows, nzs)
    wait_rows(frow, 0, (X - 1) * xrows, nxs)
    wait_rows(frow, 0, X * xrows, ncs)
    wait_rows(az, 0, (Z - 1) * Y, azs)
    wait_rows(ans, 0, (X - 1) * 8, axs)


def finish(dims, frow, fpart, ans, lab, slab, cent, table_hbm, cos_hbm, sim_hbm,
           table, cos_out, sim_out, put):
    Z, Y, X = dims
    nyz = Z * Y
    chips = nyz * X
    trows, width = cent.shape
    half_t = width // 256
    dp, x, core = position()
    rows = lab.shape[1]

    low, high = [], []
    for t in range(half_t):
        a = frow[pl.ds(t, chips, stride=half_t), :]
        b = fpart[pl.ds(t, chips, stride=half_t), :]
        low.append(jnp.where(core == 0, a, b))
        high.append(jnp.where(core == 0, b, a))
    full = jnp.concatenate(low + high, axis=1)
    row_id = (dp * X + x) * trows + iota((trows, chips), 0)
    hit = jnp.where(row_id == slab[...], 1.0, 0.0)
    named = jnp.sum(hit, axis=1, keepdims=True) > 0.5
    table[...] = jnp.where(named, select_rows(hit.astype(bf16), full), cent[...])
    pairs = [(cos_out, cos_hbm), (sim_out, sim_hbm)]
    part = trows // 4
    pairs += [
        (table.at[pl.ds(i * part, part)], table_hbm.at[pl.ds(i * part, part)]) for i in range(4)]
    puts = [pltpu.make_async_copy(src, dst, put.at[i]) for i, (src, dst) in enumerate(pairs)]
    for copy in puts[2:]:
        copy.start()

    lrow = lab[...]
    rank = ranks(lrow)
    spot = (lrow // nyz) * 128 + lrow % nyz
    member = jnp.where(iota((X * 128, rows), 0) == spot, 1.0, 0.0).astype(bf16)
    got = jnp.concatenate([ans[i * 8:(i + 1) * 8, :] for i in range(X)], axis=1)
    got = jnp.concatenate([got, jnp.zeros_like(got)], axis=0)
    got = sum(jnp.dot(p, member, preferred_element_type=f32) for p in split3(got))
    sim_out[...] = jnp.where(rank == 0, got[0:1, :], got[2:3, :])
    cos_out[...] = jnp.where(rank == 0, got[1:2, :], got[3:4, :])
    puts[0].start()
    puts[1].start()
    for copy in puts:
        copy.wait()


def local(dims, embeddings, assignment, slab_ids, centroids):
    Z, Y, X = dims
    nyz = Z * Y
    chips = nyz * X
    rows, width = embeddings.shape
    tiles = width // 128
    n_group = nyz // GROUP
    n_batch = len(plan(Z, Y)[1])
    linear = 2 * chips * tiles
    half = chips * tiles // 2
    dma = pltpu.SemaphoreType.DMA
    vmem = pl.BlockSpec(memory_space=pltpu.VMEM)
    hbm = pl.BlockSpec(memory_space=pl.ANY)
    shape = jax.ShapeDtypeStruct
    regular = pltpu.SemaphoreType.REGULAR
    labels = assignment.reshape(1, rows)

    given = pl.pallas_call(
        functools.partial(exchange, dims),
        out_shape=(
            shape((half, 128), f32),
            shape((half, 128), f32),
            shape((8 * X, 128), f32),
        ),
        in_specs=[hbm] * 2,
        out_specs=(vmem,) * 3,
        scratch_shapes=[
            pltpu.VMEM((rows, width), f32),
            pltpu.VMEM((1, rows), jnp.int32),
            pltpu.VMEM((linear, 128), f32),
            pltpu.VMEM((linear, 128), f32),
            pltpu.VMEM((linear, 128), f32),
            pltpu.VMEM((linear, 128), f32),
            pltpu.VMEM((linear, 128), f32),
            pltpu.VMEM((4 * chips + 16, width), bf16),
            pltpu.VMEM((4 * chips + 16, width), bf16),
            pltpu.VMEM((width, 2 * chips), bf16),
            pltpu.VMEM((width, 2 * chips), bf16),
            pltpu.VMEM((4 * chips, 128), f32),
            pltpu.VMEM((max(nyz, 8 * X), 128), f32),
            pltpu.VMEM((nyz, 128), f32),
            pltpu.VMEM((nyz, 128), f32),
            pltpu.VMEM((nyz, 128), f32),
            regular, regular,
            dma((5,)), dma, dma((n_batch,)),
            dma, dma((n_group,)), dma, dma((n_group,)),
            dma, dma, dma, dma, dma, dma((6,)), dma, dma((X,)),
            dma, dma, dma, dma, dma, dma,
        ],
        compiler_params=pltpu.CompilerParams(
            collective_id=0, has_side_effects=True, vmem_limit_bytes=KERNEL_BYTES),
    )(embeddings, labels)

    table, cos, sim = pl.pallas_call(
        functools.partial(finish, dims),
        out_shape=(
            shape(centroids.shape, f32),
            shape((1, rows), f32),
            shape((1, rows), f32),
        ),
        in_specs=[vmem] * 6,
        out_specs=(hbm,) * 3,
        scratch_shapes=[
            pltpu.VMEM(centroids.shape, f32),
            pltpu.VMEM((1, rows), f32),
            pltpu.VMEM((1, rows), f32),
            dma((6,)),
        ],
        compiler_params=pltpu.CompilerParams(vmem_limit_bytes=32 * 2**20),
    )(*given, labels, slab_ids.reshape(1, chips), centroids)
    return table, cos.reshape(rows), sim.reshape(rows)


def solution(mesh, dims=(Z, Y, X)):
    placed = (P(("dp", "cent"), None), P(("dp", "cent"), None), P(), P(("dp", "cent"), None))
    return jax.shard_map(
        functools.partial(local, dims),
        mesh=mesh,
        in_specs=placed,
        out_specs=(P(("dp", "cent"), None), P(("dp", "cent")), P(("dp", "cent"))),
        check_vma=False,
    )
```

```python
import functools

import jax
import jax.numpy as jnp
from jax import lax
from jax.experimental import pallas as pl
from jax.experimental.pallas import tpu as pltpu
from jax.sharding import PartitionSpec as P

epsilon = 1e-06
Z, Y, X = 8, 8, 4
GROUP = 8
KERNEL_BYTES = 105 * 2**19
SENTINEL = 4.0
STRIDE = 37
MESH = pl.DeviceIdType.MESH
f32, bf16 = jnp.float32, jnp.bfloat16


def split3(v):
    hi = v.astype(bf16)
    rest = v - hi.astype(f32)
    mid = rest.astype(bf16)
    lo = (rest - mid.astype(f32)).astype(bf16)
    return hi, mid, lo


def select_rows(onehot, v):
    hi, mid, lo = split3(v)
    dot = functools.partial(jnp.dot, preferred_element_type=f32)
    return dot(onehot, hi) + dot(onehot, mid) + dot(onehot, lo)


def iota(shape, axis):
    return lax.broadcasted_iota(jnp.int32, shape, axis)


def position():
    dp = lax.axis_index("dp")
    return dp, lax.axis_index("cent"), dp % 2


def wait_rows(buf, start, count, sem):
    part = buf.at[pl.ds(start, count)]
    pltpu.make_async_copy(part, part, sem).wait()


def ranks(lrow):
    rows = lrow.shape[1]
    lcol = jnp.broadcast_to(lrow.astype(f32), (128, rows)).T[:, 0:1].astype(jnp.int32)
    earlier = (lcol == lrow) & (iota((rows, rows), 0) < iota((rows, rows), 1))
    return jnp.sum(jnp.where(earlier, 1.0, 0.0), axis=0, keepdims=True).astype(jnp.int32)


def exchange(dims, emb_hbm, lab_hbm, slab, frow, fpart, ans,
             emb, lab, send, recv, other, khi, klo, qht, qlt, bias,
             abuf, ay, ab, az,
             line_sem, plane_sem, load, fs, fr, ps, pr,
             nys, nyr, nzs, nzr, nxs, nxr, ncs, ncr, ays, ayr, azs, azr, axs, axr):
    Z, Y, X = dims
    nyz = Z * Y
    chips = nyz * X
    n_group = nyz // GROUP
    rows, width = emb.shape
    tiles = width // 128
    half_t = tiles // 2
    msg = 2 * tiles
    own = 2 * chips
    back = pow(STRIDE, -1, nyz)

    loads = [pltpu.make_async_copy(lab_hbm, lab, load.at[0])]
    part = rows // 4
    loads += [
        pltpu.make_async_copy(
            emb_hbm.at[pl.ds(i * part, part)], emb.at[pl.ds(i * part, part)], load.at[1 + i])
        for i in range(4)
    ]
    for copy in loads:
        copy.start()

    dp, x, core = position()
    yz = dp // 2
    y = yz % Y
    z = yz // Y
    me = x * nyz + yz
    zs = [(z + d) % Z for d in range(Z)]
    ys = [(y + d) % Y for d in range(Y)]
    partner = (yz * 2 + 1 - core, x)

    def at(dz, dy, dx=0):
        return ((zs[dz % Z] * Y + ys[dy % Y]) * 2 + core, (x + dx) % X)

    def signal(sem, where):
        pl.semaphore_signal(sem, inc=1, device_id=where, device_id_type=MESH)

    def start(src, dst, send_sem, recv_sem, where):
        pltpu.make_async_remote_copy(
            src_ref=src, dst_ref=dst, send_sem=send_sem, recv_sem=recv_sem,
            device_id=where, device_id_type=MESH,
        ).start()

    barrier = pltpu.get_barrier_semaphore()
    for d in range(1, Z):
        signal(barrier, at(d, 0))
    for d in range(1, Y):
        signal(barrier, at(0, d))
    for d in range(1, X):
        signal(barrier, at(0, 0, d))
    signal(barrier, partner)

    loads[0].wait()
    lrow = lab[...]
    rank = ranks(lrow)
    lx, lyz = lrow // nyz, lrow % nyz
    code = ((lyz // Y + Z - z) % Z) * Y + (lyz % Y + Y - y) % Y
    target = 2 * (((code * back) % nyz) * X + (lx + X - x) % X) + rank

    pl.semaphore_wait(barrier, Z + Y + X - 2)
    for d in range(1, Y):
        signal(line_sem, at(0, d))

    for copy in loads[1:]:
        copy.wait()
    e = emb[...]
    unit = e * lax.rsqrt(jnp.sum(e * e, axis=1, keepdims=True) + epsilon)
    parts = split3(unit)

    n_chunk = min(4, n_group)
    chunk = own // n_chunk
    chunk_q = nyz // n_chunk

    def fill(i):
        low = i * chunk
        place = jnp.where(iota((chunk, rows), 0) + low == target, 1.0, 0.0)
        filled = jnp.sum(place, axis=1, keepdims=True) > 0.5
        place = place.astype(bf16)
        slots = sum(jnp.dot(place, p, preferred_element_type=f32) for p in parts)
        slots = jnp.where(filled, slots, SENTINEL)
        for t in range(tiles):
            send[pl.ds(low * tiles + t, chunk, stride=tiles), :] = (
                slots[:, t * 128:(t + 1) * 128])

    def straight(q, dx):
        w = (q * STRIDE) % nyz
        where = (((z + w // Y) % Z * Y + (y + w % Y) % Y) * 2 + core, (x + dx) % X)
        piece = pl.ds((q * X + dx) * msg, msg)
        start(send.at[piece], recv.at[piece], fs, fr.at[q // GROUP], where)

    def straight_all(first, last, dxs):
        def step(q, carry):
            for dx in dxs:
                straight(q, dx)
            return carry
        lax.fori_loop(first, last, step, 0)

    fill(0)
    pl.semaphore_wait(line_sem, Y - 1)
    for d in range(1, X):
        signal(plane_sem, at(0, 0, d))
    straight_all(1, chunk_q, [0])
    recv[0:msg, :] = send[0:msg, :]
    fill(1)
    pl.semaphore_wait(plane_sem, X - 1)
    straight_all(0, chunk_q, range(1, X))
    for i in range(1, n_chunk):
        if i > 1:
            fill(i)
        straight_all(i * chunk_q, (i + 1) * chunk_q, range(X))

    grows = GROUP * X * msg
    krows = GROUP * X * 2

    def take(buf, g, base, total):
        columns = []
        dead = None
        for t in range(tiles):
            pieces = []
            for dx in range(X):
                for s in range(2):
                    first = g * grows + dx * msg + s * tiles + t
                    pieces.append(buf[pl.ds(first, GROUP, stride=X * msg), :])
            v = jnp.concatenate(pieces, axis=0)
            if dead is None:
                dead = v > 2.0
                bias[pl.ds(base + g * krows, krows), :] = jnp.where(dead, -4.0, 0.0)
            v = jnp.where(dead, 0.0, v)
            hi = v.astype(bf16)
            lo = (v - hi.astype(f32)).astype(bf16)
            khi[pl.ds(base + g * krows, krows), t * 128:(t + 1) * 128] = hi
            klo[pl.ds(base + g * krows, krows), t * 128:(t + 1) * 128] = lo
            columns.append(jnp.sum(v, axis=0, keepdims=True))
        return total + jnp.concatenate(columns, axis=1)

    mine = jnp.zeros((1, width), f32)
    theirs = jnp.zeros((1, width), f32)
    for g in range(n_group):
        missing = msg if g == 0 else 0
        wait_rows(recv, g * grows + missing, grows - missing, fr.at[g])
        piece = pl.ds(g * grows, grows)
        start(recv.at[piece], other.at[piece], ps, pr.at[g], partner)
        mine = take(recv, g, 0, mine)
        block = g * krows // 128
        if g == n_group - 1 or (g + 1) * krows // 128 > block:
            top = pl.ds(block * 128, min(128, own))
            for t in range(tiles):
                lanes = pl.ds(t * 128, 128)
                qht[lanes, top] = khi[top, lanes].astype(f32).T.astype(bf16)
                qlt[lanes, top] = klo[top, lanes].astype(f32).T.astype(bf16)
        wait_rows(other, g * grows, grows, pr.at[g])
        theirs = take(other, g, own, theirs)

    sums = mine + theirs
    fresh = sums * lax.rsqrt(jnp.sum(sums * sums, axis=1, keepdims=True) + epsilon)
    for t in range(half_t):
        a = fresh[:, t * 128:(t + 1) * 128]
        b = fresh[:, (half_t + t) * 128:(half_t + t + 1) * 128]
        frow[pl.ds(me * half_t + t, 1), :] = jnp.where(core == 0, a, b)
    piece = pl.ds(me * half_t, half_t)
    for d in range(1, Y):
        start(frow.at[piece], frow.at[piece], nys, nyr, at(0, d))
    fh = fresh.astype(bf16)
    khi[2 * own:2 * own + 16, :] = jnp.broadcast_to(fresh, (16, width)).astype(bf16)
    klo[2 * own:2 * own + 16, :] = jnp.broadcast_to(
        fresh - fh.astype(f32), (16, width)).astype(bf16)

    def product(first, count):
        kh = khi[first:first + count, :]
        kl = klo[first:first + count, :]
        dot = functools.partial(jnp.dot, preferred_element_type=f32)
        return dot(kh, qht[...]) + dot(kh, qlt[...]) + dot(kl, qht[...])

    def closest(s, first):
        off = bias[first:first + own, :]
        s = s + (jnp.concatenate([off] * (own // 128), axis=1) if own > 128 else off[:, :own])
        if first == 0:
            s = jnp.where(iota((own, own), 0) == iota((own, own), 1), -4.0, s)
        return jnp.max(s, axis=0, keepdims=True)

    best = jnp.maximum(closest(product(0, own), 0), -1.0)

    yrows = Y * half_t
    wait_rows(frow, 0, (Y - 1) * half_t, nyr)
    piece = pl.ds((x * nyz + z * Y) * half_t, yrows)
    for d in range(1, Z):
        start(frow.at[piece], frow.at[piece], nzs, nzr, at(d, 0))

    s = product(own, own + 16)
    best = jnp.maximum(best, closest(s[:own, :], own))
    cos = s[own:own + 1, :]

    xs = (iota((128, own), 1) // GROUP) % (2 * X)
    lane_of = (xs // 2) * 8 + (xs % 2) * 2
    j = iota((128, own), 0)
    spread = jnp.where(j == lane_of, best, jnp.where(j == lane_of + 1, cos, 0.0))
    spread = spread.T.reshape(n_group, 2 * X, GROUP, 128)
    spread = jnp.sum(spread, axis=1).reshape(nyz, 128)
    for q in range(nyz):
        dz, dy = (q * STRIDE) % nyz // Y, (q * STRIDE) % nyz % Y
        abuf[dy * Z + dz:dy * Z + dz + 1, :] = spread[q:q + 1, :]
    for d in range(1, Y):
        start(abuf.at[pl.ds(d * Z, Z)], ay.at[pl.ds(y * Z, Z)], ays, ayr, at(0, -d))
    ay[pl.ds(y * Z, Z), :] = abuf[0:Z, :]

    xrows = nyz * half_t
    hrows = xrows // 2

    def block_of(dx, half):
        return pl.ds(((x + dx) % X) * xrows + half * hrows, hrows)

    def along(dx, half, sem, to):
        piece = block_of(dx, half)
        start(frow.at[piece], frow.at[piece], nxs, nxr.at[sem], at(0, 0, to))

    def pass_on(dx):
        piece = pl.ds(((x + dx) % X) * xrows, xrows)
        start(frow.at[piece], fpart.at[piece], ncs, ncr.at[dx], partner)

    def landed(dx, half, sem):
        wait_rows(frow, ((x + dx) % X) * xrows + half * hrows, hrows, nxr.at[sem])

    wait_rows(frow, 0, (Z - 1) * yrows, nzr)
    along(0, 0, 0, 1)
    if X > 2:
        along(0, 1, 2, X - 1)
    along(0, 1, 1, 1)
    if X > 2:
        along(0, 0, 3, X - 1)
    pass_on(0)
    if X > 2:
        landed(X - 1, 0, 0)
        along(X - 1, 0, 4, 1)
        landed(1, 1, 2)
        along(1, 1, 5, X - 1)

    wait_rows(ay, 0, (Y - 1) * Z, ayr)
    for dz in range(Z):
        ab[dz * Y:(dz + 1) * Y, :] = ay[pl.ds(dz, Y, stride=Z), :]
    for d in range(1, Z):
        start(ab.at[pl.ds(d * Y, Y)], az.at[pl.ds(z * Y, Y)], azs, azr, at(-d, 0))
    az[pl.ds(z * Y, Y), :] = ab[0:Y, :]

    if X > 2:
        landed(X - 1, 1, 1)
        pass_on(X - 1)
        landed(1, 0, 3)
        pass_on(1)
    else:
        landed(1, 0, 0)
        landed(1, 1, 1)
        pass_on(1)

    wait_rows(az, 0, (Z - 1) * Y, azr)
    wait_rows(ay, 0, (Y - 1) * Z, ays)
    turned = jnp.concatenate([az[...], jnp.zeros((128 - nyz, 128), f32)], axis=0).T
    abuf[0:8 * X, :] = turned[0:8 * X, :]
    for d in range(1, X):
        start(abuf.at[pl.ds(d * 8, 8)], ans.at[pl.ds(x * 8, 8)], axs, axr, at(0, 0, X - d))
    ans[pl.ds(x * 8, 8), :] = abuf[0:8, :]

    if X > 2:
        landed(2, 0, 4)
        landed(2, 1, 5)
        pass_on(2)
    for dx in range(X):
        wait_rows(fpart, ((x + dx) % X) * xrows, xrows, ncr.at[dx])
    wait_rows(ans, 0, (X - 1) * 8, axr)

    wait_rows(send, 0, (chips - 1) * msg, fs)
    wait_rows(recv, 0, n_group * grows, ps)
    wait_rows(frow, 0, (Y - 1) * half_t, nys)
    wait_rows(frow, 0, (Z - 1) * yrows, nzs)
    wait_rows(frow, 0, (X - 1) * xrows, nxs)
    wait_rows(frow, 0, X * xrows, ncs)
    wait_rows(az, 0, (Z - 1) * Y, azs)
    wait_rows(ans, 0, (X - 1) * 8, axs)


def finish(dims, frow, fpart, ans, lab, slab, cent, table_hbm, cos_hbm, sim_hbm,
           table, cos_out, sim_out, put):
    Z, Y, X = dims
    nyz = Z * Y
    chips = nyz * X
    trows, width = cent.shape
    half_t = width // 256
    dp, x, core = position()
    rows = lab.shape[1]

    low, high = [], []
    for t in range(half_t):
        a = frow[pl.ds(t, chips, stride=half_t), :]
        b = fpart[pl.ds(t, chips, stride=half_t), :]
        low.append(jnp.where(core == 0, a, b))
        high.append(jnp.where(core == 0, b, a))
    full = jnp.concatenate(low + high, axis=1)
    row_id = (dp * X + x) * trows + iota((trows, chips), 0)
    hit = jnp.where(row_id == slab[...], 1.0, 0.0)
    named = jnp.sum(hit, axis=1, keepdims=True) > 0.5
    table[...] = jnp.where(named, select_rows(hit.astype(bf16), full), cent[...])
    pairs = [(cos_out, cos_hbm), (sim_out, sim_hbm)]
    part = trows // 4
    pairs += [
        (table.at[pl.ds(i * part, part)], table_hbm.at[pl.ds(i * part, part)]) for i in range(4)]
    puts = [pltpu.make_async_copy(src, dst, put.at[i]) for i, (src, dst) in enumerate(pairs)]
    for copy in puts[2:]:
        copy.start()

    lrow = lab[...]
    rank = ranks(lrow)
    spot = (lrow // nyz) * 128 + lrow % nyz
    member = jnp.where(iota((X * 128, rows), 0) == spot, 1.0, 0.0).astype(bf16)
    got = jnp.concatenate([ans[i * 8:(i + 1) * 8, :] for i in range(X)], axis=1)
    got = jnp.concatenate([got, jnp.zeros_like(got)], axis=0)
    got = sum(jnp.dot(p, member, preferred_element_type=f32) for p in split3(got))
    sim_out[...] = jnp.where(rank == 0, got[0:1, :], got[2:3, :])
    cos_out[...] = jnp.where(rank == 0, got[1:2, :], got[3:4, :])
    puts[0].start()
    puts[1].start()
    for copy in puts:
        copy.wait()


def local(dims, embeddings, assignment, slab_ids, centroids):
    Z, Y, X = dims
    nyz = Z * Y
    chips = nyz * X
    rows, width = embeddings.shape
    tiles = width // 128
    n_group = nyz // GROUP
    linear = 2 * chips * tiles
    half = chips * tiles // 2
    dma = pltpu.SemaphoreType.DMA
    vmem = pl.BlockSpec(memory_space=pltpu.VMEM)
    hbm = pl.BlockSpec(memory_space=pl.ANY)
    shape = jax.ShapeDtypeStruct
    regular = pltpu.SemaphoreType.REGULAR
    labels = assignment.reshape(1, rows)
    slabs = slab_ids.reshape(1, chips)

    given = pl.pallas_call(
        functools.partial(exchange, dims),
        out_shape=(
            shape((half, 128), f32),
            shape((half, 128), f32),
            shape((8 * X, 128), f32),
        ),
        in_specs=[hbm] * 2 + [vmem],
        out_specs=(vmem,) * 3,
        scratch_shapes=[
            pltpu.VMEM((rows, width), f32),
            pltpu.VMEM((1, rows), jnp.int32),
            pltpu.VMEM((linear, 128), f32),
            pltpu.VMEM((linear, 128), f32),
            pltpu.VMEM((linear, 128), f32),
            pltpu.VMEM((4 * chips + 16, width), bf16),
            pltpu.VMEM((4 * chips + 16, width), bf16),
            pltpu.VMEM((width, 2 * chips), bf16),
            pltpu.VMEM((width, 2 * chips), bf16),
            pltpu.VMEM((4 * chips, 128), f32),
            pltpu.VMEM((max(nyz, 8 * X), 128), f32),
            pltpu.VMEM((nyz, 128), f32),
            pltpu.VMEM((nyz, 128), f32),
            pltpu.VMEM((nyz, 128), f32),
            regular, regular,
            dma((5,)),
            dma, dma((n_group,)), dma, dma((n_group,)),
            dma, dma, dma, dma, dma, dma((6,)), dma, dma((X,)),
            dma, dma, dma, dma, dma, dma,
        ],
        compiler_params=pltpu.CompilerParams(
            collective_id=0, has_side_effects=True, vmem_limit_bytes=KERNEL_BYTES),
    )(embeddings, labels, slabs)

    table, cos, sim = pl.pallas_call(
        functools.partial(finish, dims),
        out_shape=(
            shape(centroids.shape, f32),
            shape((1, rows), f32),
            shape((1, rows), f32),
        ),
        in_specs=[vmem] * 6,
        out_specs=(hbm,) * 3,
        scratch_shapes=[
            pltpu.VMEM(centroids.shape, f32),
            pltpu.VMEM((1, rows), f32),
            pltpu.VMEM((1, rows), f32),
            dma((6,)),
        ],
        compiler_params=pltpu.CompilerParams(vmem_limit_bytes=32 * 2**20),
    )(*given, labels, slabs, centroids)
    return table, cos.reshape(rows), sim.reshape(rows)


def solution(mesh, dims=(Z, Y, X)):
    placed = (P(("dp", "cent"), None), P(("dp", "cent"), None), P(), P(("dp", "cent"), None))
    return jax.shard_map(
        functools.partial(local, dims),
        mesh=mesh,
        in_specs=placed,
        out_specs=(P(("dp", "cent"), None), P(("dp", "cent")), P(("dp", "cent"))),
        check_vma=False,
    )
```

```python
import functools

import jax
import jax.numpy as jnp
from jax import lax
from jax.experimental import pallas as pl
from jax.experimental.pallas import tpu as pltpu
from jax.sharding import PartitionSpec as P

epsilon = 1e-06
Z, Y, X = 8, 8, 4
GROUP = 8
KERNEL_BYTES = 105 * 2**19
SENTINEL = 4.0
STRIDE = 37
MESH = pl.DeviceIdType.MESH
f32, bf16 = jnp.float32, jnp.bfloat16


def split3(v):
    hi = v.astype(bf16)
    rest = v - hi.astype(f32)
    mid = rest.astype(bf16)
    lo = (rest - mid.astype(f32)).astype(bf16)
    return hi, mid, lo


def select_rows(onehot, v):
    hi, mid, lo = split3(v)
    dot = functools.partial(jnp.dot, preferred_element_type=f32)
    return dot(onehot, hi) + dot(onehot, mid) + dot(onehot, lo)


def iota(shape, axis):
    return lax.broadcasted_iota(jnp.int32, shape, axis)


def position():
    dp = lax.axis_index("dp")
    return dp, lax.axis_index("cent"), dp % 2


def wait_rows(buf, start, count, sem):
    part = buf.at[pl.ds(start, count)]
    pltpu.make_async_copy(part, part, sem).wait()


def ranks(lrow):
    rows = lrow.shape[1]
    lcol = jnp.broadcast_to(lrow.astype(f32), (128, rows)).T[:, 0:1].astype(jnp.int32)
    earlier = (lcol == lrow) & (iota((rows, rows), 0) < iota((rows, rows), 1))
    return jnp.sum(jnp.where(earlier, 1.0, 0.0), axis=0, keepdims=True).astype(jnp.int32)


def exchange(dims, emb_hbm, lab_hbm, slab, frow, fpart, ans,
             emb, lab, send, stage, out, recv, other, keys, queries, bias,
             abuf, ay, ab, az,
             line_sem, load, gs, gr, fs, fr, ps, pr,
             nys, nyr, nzs, nzr, nxs, nxr, ncs, ncr, ays, ayr, azs, azr, axs, axr):
    Z, Y, X = dims
    nyz = Z * Y
    chips = nyz * X
    n_group = nyz // GROUP
    rows, width = emb.shape
    tiles = width // 128
    half_t = tiles // 2
    msg = 2 * tiles
    own = 2 * chips
    back = pow(STRIDE, -1, nyz)

    loads = [pltpu.make_async_copy(lab_hbm, lab, load.at[0])]
    part = rows // 4
    loads += [
        pltpu.make_async_copy(
            emb_hbm.at[pl.ds(i * part, part)], emb.at[pl.ds(i * part, part)], load.at[1 + i])
        for i in range(4)
    ]
    for copy in loads:
        copy.start()

    dp, x, core = position()
    yz = dp // 2
    y = yz % Y
    z = yz // Y
    me = x * nyz + yz
    zs = [(z + d) % Z for d in range(Z)]
    ys = [(y + d) % Y for d in range(Y)]
    partner = (yz * 2 + 1 - core, x)

    def at(dz, dy, dx=0):
        return ((zs[dz % Z] * Y + ys[dy % Y]) * 2 + core, (x + dx) % X)

    def signal(sem, where):
        pl.semaphore_signal(sem, inc=1, device_id=where, device_id_type=MESH)

    def start(src, dst, send_sem, recv_sem, where):
        pltpu.make_async_remote_copy(
            src_ref=src, dst_ref=dst, send_sem=send_sem, recv_sem=recv_sem,
            device_id=where, device_id_type=MESH,
        ).start()

    barrier = pltpu.get_barrier_semaphore()
    for d in range(1, Z):
        signal(barrier, at(d, 0))
    for d in range(1, Y):
        signal(barrier, at(0, d))
    for d in range(1, X):
        signal(barrier, at(0, 0, d))
    signal(barrier, partner)

    loads[0].wait()
    lrow = lab[...]
    rank = ranks(lrow)
    lx, lyz = lrow // nyz, lrow % nyz
    code = ((lyz // Y + Z - z) % Z) * Y + (lyz % Y + Y - y) % Y
    q_row = (code * back) % nyz
    target = 2 * (((q_row // GROUP) * X + (lx + X - x) % X) * GROUP + q_row % GROUP) + rank

    pl.semaphore_wait(barrier, Z + Y + X - 2)
    for d in range(1, Y):
        signal(line_sem, at(0, d))

    for copy in loads[1:]:
        copy.wait()
    e = emb[...]
    unit = e * lax.rsqrt(jnp.sum(e * e, axis=1, keepdims=True) + epsilon)
    parts = split3(unit)

    n_chunk = min(4, n_group)
    chunk = own // n_chunk
    chunk_q = nyz // n_chunk

    def fill(i):
        low = i * chunk
        place = jnp.where(iota((chunk, rows), 0) + low == target, 1.0, 0.0)
        filled = jnp.sum(place, axis=1, keepdims=True) > 0.5
        place = place.astype(bf16)
        slots = sum(jnp.dot(place, p, preferred_element_type=f32) for p in parts)
        slots = jnp.where(filled, slots, SENTINEL)
        for t in range(tiles):
            send[pl.ds(low * tiles + t, chunk, stride=tiles), :] = (
                slots[:, t * 128:(t + 1) * 128])

    def owner_at(q):
        w = (q * STRIDE) % nyz
        return ((z + w // Y) % Z * Y + (y + w % Y) % Y) * 2 + core, x

    def straight(q, carry):
        slot = (q // GROUP * X) * GROUP + q % GROUP
        start(send.at[pl.ds(slot * msg, msg)], recv.at[pl.ds(q * X * msg, msg)],
              fs, fr.at[q // GROUP], owner_at(q))
        return carry

    def onward(q, carry):
        piece = pl.ds((q * X + 1) * msg, (X - 1) * msg)
        start(out.at[piece], recv.at[piece], fs, fr.at[q // GROUP], owner_at(q))
        return carry

    block = GROUP * msg
    for i in range(n_chunk):
        fill(i)
        for g in range(i * chunk_q // GROUP, (i + 1) * chunk_q // GROUP):
            for dx in range(1, X):
                start(send.at[pl.ds((g * X + dx) * block, block)],
                      stage.at[pl.ds((g * (X - 1) + dx - 1) * block, block)],
                      gs, gr.at[g], at(0, 0, dx))
        if i == 0:
            pl.semaphore_wait(line_sem, Y - 1)
            recv[0:msg, :] = send[0:msg, :]
        lax.fori_loop(max(i * chunk_q, 1), (i + 1) * chunk_q, straight, 0)
    for g in range(n_group):
        wait_rows(stage, g * (X - 1) * block, (X - 1) * block, gr.at[g])
        for j in range(GROUP):
            q = g * GROUP + j
            into = recv if q == 0 else out
            for dx in range(1, X):
                into[pl.ds((q * X + dx) * msg, msg), :] = (
                    stage[pl.ds((g * (X - 1) + dx - 1) * block + j * msg, msg), :])
        lax.fori_loop(max(g * GROUP, 1), (g + 1) * GROUP, onward, 0)

    grows = GROUP * X * msg
    krows = GROUP * X * 2

    def take(buf, g, base, total):
        columns = []
        dead = None
        for t in range(tiles):
            pieces = []
            for dx in range(X):
                for s in range(2):
                    first = g * grows + dx * msg + s * tiles + t
                    pieces.append(buf[pl.ds(first, GROUP, stride=X * msg), :])
            v = jnp.concatenate(pieces, axis=0)
            if dead is None:
                dead = v > 2.0
                bias[pl.ds(base + g * krows, krows), :] = jnp.where(dead, -4.0, 0.0)
            v = jnp.where(dead, 0.0, v)
            hi = v.astype(bf16)
            lo = (v - hi.astype(f32)).astype(bf16)
            for i, v_part in enumerate((hi, lo, hi)):
                keys[pl.ds(base + g * krows, krows), pl.ds(i * width + t * 128, 128)] = v_part
            columns.append(jnp.sum(v, axis=0, keepdims=True))
        return total + jnp.concatenate(columns, axis=1)

    mine = jnp.zeros((1, width), f32)
    theirs = jnp.zeros((1, width), f32)
    for g in range(n_group):
        missing = X * msg if g == 0 else 0
        wait_rows(recv, g * grows + missing, grows - missing, fr.at[g])
        piece = pl.ds(g * grows, grows)
        start(recv.at[piece], other.at[piece], ps, pr.at[g], partner)
        mine = take(recv, g, 0, mine)
        tile = g * krows // 128
        if g == n_group - 1 or (g + 1) * krows // 128 > tile:
            top = pl.ds(tile * 128, min(128, own))
            for t in range(tiles):
                hi = keys[top, pl.ds(t * 128, 128)].astype(f32).T.astype(bf16)
                lo = keys[top, pl.ds(width + t * 128, 128)].astype(f32).T.astype(bf16)
                for i, v_part in enumerate((hi, hi, lo)):
                    queries[pl.ds(i * width + t * 128, 128), top] = v_part
        wait_rows(other, g * grows, grows, pr.at[g])
        theirs = take(other, g, own, theirs)

    sums = mine + theirs
    fresh = sums * lax.rsqrt(jnp.sum(sums * sums, axis=1, keepdims=True) + epsilon)
    for t in range(half_t):
        a = fresh[:, t * 128:(t + 1) * 128]
        b = fresh[:, (half_t + t) * 128:(half_t + t + 1) * 128]
        frow[pl.ds(me * half_t + t, 1), :] = jnp.where(core == 0, a, b)
    piece = pl.ds(me * half_t, half_t)
    for d in range(1, Y):
        start(frow.at[piece], frow.at[piece], nys, nyr, at(0, d))
    fh = fresh.astype(bf16)
    fl = jnp.broadcast_to(fresh - fh.astype(f32), (16, width)).astype(bf16)
    fh = jnp.broadcast_to(fresh, (16, width)).astype(bf16)
    keys[2 * own:2 * own + 16, :] = jnp.concatenate([fh, fl, fh], axis=1)

    xrows = nyz * half_t
    hrows = xrows // 2

    def block_of(dx, half):
        return pl.ds(((x + dx) % X) * xrows + half * hrows, hrows)

    def along(dx, half, sem, to):
        piece = block_of(dx, half)
        start(frow.at[piece], frow.at[piece], nxs, nxr.at[sem], at(0, 0, to))

    def pass_on(dx):
        piece = pl.ds(((x + dx) % X) * xrows, xrows)
        start(frow.at[piece], fpart.at[piece], ncs, ncr.at[dx], partner)

    def landed(dx, half, sem):
        wait_rows(frow, ((x + dx) % X) * xrows + half * hrows, hrows, nxr.at[sem])

    quarter = own // 2

    def product(first, count):
        return jnp.dot(keys[first:first + count, :], queries[...], preferred_element_type=f32)

    def closest(s, first):
        off = bias[first:first + quarter, :]
        s = s + (jnp.concatenate([off] * (own // 128), axis=1) if own > 128 else off[:, :own])
        if first < own:
            itself = iota((quarter, own), 0) + first == iota((quarter, own), 1)
            s = jnp.where(itself, -4.0, s)
        return jnp.max(s, axis=0, keepdims=True)

    best = jnp.maximum(closest(product(0, quarter), 0), -1.0)

    yrows = Y * half_t
    wait_rows(frow, 0, (Y - 1) * half_t, nyr)
    piece = pl.ds((x * nyz + z * Y) * half_t, yrows)
    for d in range(1, Z):
        start(frow.at[piece], frow.at[piece], nzs, nzr, at(d, 0))

    best = jnp.maximum(best, closest(product(quarter, quarter), quarter))
    best = jnp.maximum(best, closest(product(own, quarter), own))

    wait_rows(frow, 0, (Z - 1) * yrows, nzr)
    along(0, 0, 0, 1)
    if X > 2:
        along(0, 1, 2, X - 1)
    along(0, 1, 1, 1)
    if X > 2:
        along(0, 0, 3, X - 1)
    pass_on(0)

    s = product(own + quarter, quarter + 16)
    best = jnp.maximum(best, closest(s[:quarter, :], own + quarter))
    cos = s[quarter:quarter + 1, :]

    xs = (iota((128, own), 1) // GROUP) % (2 * X)
    lane_of = (xs // 2) * 8 + (xs % 2) * 2
    j = iota((128, own), 0)
    spread = jnp.where(j == lane_of, best, jnp.where(j == lane_of + 1, cos, 0.0))
    spread = spread.T.reshape(n_group, 2 * X, GROUP, 128)
    spread = jnp.sum(spread, axis=1).reshape(nyz, 128)
    for q in range(nyz):
        dz, dy = (q * STRIDE) % nyz // Y, (q * STRIDE) % nyz % Y
        abuf[dy * Z + dz:dy * Z + dz + 1, :] = spread[q:q + 1, :]
    for d in range(1, Y):
        start(abuf.at[pl.ds(d * Z, Z)], ay.at[pl.ds(y * Z, Z)], ays, ayr, at(0, -d))
    ay[pl.ds(y * Z, Z), :] = abuf[0:Z, :]

    if X > 2:
        landed(X - 1, 0, 0)
        along(X - 1, 0, 4, 1)
        landed(1, 1, 2)
        along(1, 1, 5, X - 1)

    wait_rows(ay, 0, (Y - 1) * Z, ayr)
    for dz in range(Z):
        ab[dz * Y:(dz + 1) * Y, :] = ay[pl.ds(dz, Y, stride=Z), :]
    for d in range(1, Z):
        start(ab.at[pl.ds(d * Y, Y)], az.at[pl.ds(z * Y, Y)], azs, azr, at(-d, 0))
    az[pl.ds(z * Y, Y), :] = ab[0:Y, :]

    if X > 2:
        landed(X - 1, 1, 1)
        pass_on(X - 1)
        landed(1, 0, 3)
        pass_on(1)
    else:
        landed(1, 0, 0)
        landed(1, 1, 1)
        pass_on(1)

    wait_rows(az, 0, (Z - 1) * Y, azr)
    wait_rows(ay, 0, (Y - 1) * Z, ays)
    turned = jnp.concatenate([az[...], jnp.zeros((128 - nyz, 128), f32)], axis=0).T
    abuf[0:8 * X, :] = turned[0:8 * X, :]
    for d in range(1, X):
        start(abuf.at[pl.ds(d * 8, 8)], ans.at[pl.ds(x * 8, 8)], axs, axr, at(0, 0, X - d))
    ans[pl.ds(x * 8, 8), :] = abuf[0:8, :]

    if X > 2:
        landed(2, 0, 4)
        landed(2, 1, 5)
        pass_on(2)
    for dx in range(X):
        wait_rows(fpart, ((x + dx) % X) * xrows, xrows, ncr.at[dx])
    wait_rows(ans, 0, (X - 1) * 8, axr)

    wait_rows(send, 0, (X - 1) * nyz * msg, gs)
    wait_rows(send, 0, (nyz - 1) * X * msg, fs)
    wait_rows(recv, 0, n_group * grows, ps)
    wait_rows(frow, 0, (Y - 1) * half_t, nys)
    wait_rows(frow, 0, (Z - 1) * yrows, nzs)
    wait_rows(frow, 0, (X - 1) * xrows, nxs)
    wait_rows(frow, 0, X * xrows, ncs)
    wait_rows(az, 0, (Z - 1) * Y, azs)
    wait_rows(ans, 0, (X - 1) * 8, axs)


def finish(dims, frow, fpart, ans, lab, slab, cent, table_hbm, cos_hbm, sim_hbm,
           table, cos_out, sim_out, put):
    Z, Y, X = dims
    nyz = Z * Y
    chips = nyz * X
    trows, width = cent.shape
    half_t = width // 256
    dp, x, core = position()
    rows = lab.shape[1]

    low, high = [], []
    for t in range(half_t):
        a = frow[pl.ds(t, chips, stride=half_t), :]
        b = fpart[pl.ds(t, chips, stride=half_t), :]
        low.append(jnp.where(core == 0, a, b))
        high.append(jnp.where(core == 0, b, a))
    full = jnp.concatenate(low + high, axis=1)
    row_id = (dp * X + x) * trows + iota((trows, chips), 0)
    hit = jnp.where(row_id == slab[...], 1.0, 0.0)
    named = jnp.sum(hit, axis=1, keepdims=True) > 0.5
    table[...] = jnp.where(named, select_rows(hit.astype(bf16), full), cent[...])
    pairs = [(cos_out, cos_hbm), (sim_out, sim_hbm)]
    part = trows // 4
    pairs += [
        (table.at[pl.ds(i * part, part)], table_hbm.at[pl.ds(i * part, part)]) for i in range(4)]
    puts = [pltpu.make_async_copy(src, dst, put.at[i]) for i, (src, dst) in enumerate(pairs)]
    for copy in puts[2:]:
        copy.start()

    lrow = lab[...]
    rank = ranks(lrow)
    spot = (lrow // nyz) * 128 + lrow % nyz
    member = jnp.where(iota((X * 128, rows), 0) == spot, 1.0, 0.0).astype(bf16)
    got = jnp.concatenate([ans[i * 8:(i + 1) * 8, :] for i in range(X)], axis=1)
    got = jnp.concatenate([got, jnp.zeros_like(got)], axis=0)
    got = sum(jnp.dot(p, member, preferred_element_type=f32) for p in split3(got))
    sim_out[...] = jnp.where(rank == 0, got[0:1, :], got[2:3, :])
    cos_out[...] = jnp.where(rank == 0, got[1:2, :], got[3:4, :])
    puts[0].start()
    puts[1].start()
    for copy in puts:
        copy.wait()


def local(dims, embeddings, assignment, slab_ids, centroids):
    Z, Y, X = dims
    nyz = Z * Y
    chips = nyz * X
    rows, width = embeddings.shape
    tiles = width // 128
    n_group = nyz // GROUP
    linear = 2 * chips * tiles
    half = chips * tiles // 2
    dma = pltpu.SemaphoreType.DMA
    vmem = pl.BlockSpec(memory_space=pltpu.VMEM)
    hbm = pl.BlockSpec(memory_space=pl.ANY)
    shape = jax.ShapeDtypeStruct
    regular = pltpu.SemaphoreType.REGULAR
    labels = assignment.reshape(1, rows)
    slabs = slab_ids.reshape(1, chips)

    given = pl.pallas_call(
        functools.partial(exchange, dims),
        out_shape=(
            shape((half, 128), f32),
            shape((half, 128), f32),
            shape((8 * X, 128), f32),
        ),
        in_specs=[hbm] * 2 + [vmem],
        out_specs=(vmem,) * 3,
        scratch_shapes=[
            pltpu.VMEM((rows, width), f32),
            pltpu.VMEM((1, rows), jnp.int32),
            pltpu.VMEM((linear, 128), f32),
            pltpu.VMEM((linear // X * (X - 1), 128), f32),
            pltpu.VMEM((linear, 128), f32),
            pltpu.VMEM((linear, 128), f32),
            pltpu.VMEM((linear, 128), f32),
            pltpu.VMEM((4 * chips + 16, 3 * width), bf16),
            pltpu.VMEM((3 * width, 2 * chips), bf16),
            pltpu.VMEM((4 * chips, 128), f32),
            pltpu.VMEM((max(nyz, 8 * X), 128), f32),
            pltpu.VMEM((nyz, 128), f32),
            pltpu.VMEM((nyz, 128), f32),
            pltpu.VMEM((nyz, 128), f32),
            regular,
            dma((5,)), dma, dma((n_group,)),
            dma, dma((n_group,)), dma, dma((n_group,)),
            dma, dma, dma, dma, dma, dma((6,)), dma, dma((X,)),
            dma, dma, dma, dma, dma, dma,
        ],
        compiler_params=pltpu.CompilerParams(
            collective_id=0, has_side_effects=True, vmem_limit_bytes=KERNEL_BYTES),
    )(embeddings, labels, slabs)

    table, cos, sim = pl.pallas_call(
        functools.partial(finish, dims),
        out_shape=(
            shape(centroids.shape, f32),
            shape((1, rows), f32),
            shape((1, rows), f32),
        ),
        in_specs=[vmem] * 6,
        out_specs=(hbm,) * 3,
        scratch_shapes=[
            pltpu.VMEM(centroids.shape, f32),
            pltpu.VMEM((1, rows), f32),
            pltpu.VMEM((1, rows), f32),
            dma((6,)),
        ],
        compiler_params=pltpu.CompilerParams(vmem_limit_bytes=32 * 2**20),
    )(*given, labels, slabs, centroids)
    return table, cos.reshape(rows), sim.reshape(rows)


def solution(mesh, dims=(Z, Y, X)):
    placed = (P(("dp", "cent"), None), P(("dp", "cent"), None), P(), P(("dp", "cent"), None))
    return jax.shard_map(
        functools.partial(local, dims),
        mesh=mesh,
        in_specs=placed,
        out_specs=(P(("dp", "cent"), None), P(("dp", "cent")), P(("dp", "cent"))),
        check_vma=False,
    )
```

```python
import functools

import jax
import jax.numpy as jnp
from jax import lax
from jax.experimental import pallas as pl
from jax.experimental.pallas import tpu as pltpu
from jax.sharding import PartitionSpec as P

epsilon = 1e-06
Z, Y, X = 8, 8, 4
GROUP = 8
KERNEL_BYTES = 105 * 2**19
SENTINEL = 4.0
STRIDE = 37
MESH = pl.DeviceIdType.MESH
f32, bf16 = jnp.float32, jnp.bfloat16


def split3(v):
    hi = v.astype(bf16)
    rest = v - hi.astype(f32)
    mid = rest.astype(bf16)
    lo = (rest - mid.astype(f32)).astype(bf16)
    return hi, mid, lo


def select_rows(onehot, v):
    hi, mid, lo = split3(v)
    dot = functools.partial(jnp.dot, preferred_element_type=f32)
    return dot(onehot, hi) + dot(onehot, mid) + dot(onehot, lo)


def iota(shape, axis):
    return lax.broadcasted_iota(jnp.int32, shape, axis)


def position():
    dp = lax.axis_index("dp")
    return dp, lax.axis_index("cent"), dp % 2


def wait_rows(buf, start, count, sem):
    part = buf.at[pl.ds(start, count)]
    pltpu.make_async_copy(part, part, sem).wait()


def ranks(lrow):
    rows = lrow.shape[1]
    lcol = jnp.broadcast_to(lrow.astype(f32), (128, rows)).T[:, 0:1].astype(jnp.int32)
    earlier = (lcol == lrow) & (iota((rows, rows), 0) < iota((rows, rows), 1))
    return jnp.sum(jnp.where(earlier, 1.0, 0.0), axis=0, keepdims=True).astype(jnp.int32)


def exchange(dims, emb_hbm, lab_hbm, slab, frow, fpart, ans,
             emb, lab, send, recv, other, keys, queries, bias, part_sum,
             abuf, ay, ab, az,
             line_sem, plane_sem, load, fs, fr, ps, pr, ss, sr,
             nys, nyr, nzs, nzr, nxs, nxr, ncs, ncr, ays, ayr, azs, azr, axs, axr):
    Z, Y, X = dims
    nyz = Z * Y
    chips = nyz * X
    n_group = nyz // GROUP
    rows, width = emb.shape
    tiles = width // 128
    half_t = tiles // 2
    msg = 2 * tiles
    own = 2 * chips
    back = pow(STRIDE, -1, nyz)

    loads = [pltpu.make_async_copy(lab_hbm, lab, load.at[0])]
    part = rows // 4
    loads += [
        pltpu.make_async_copy(
            emb_hbm.at[pl.ds(i * part, part)], emb.at[pl.ds(i * part, part)], load.at[1 + i])
        for i in range(4)
    ]
    for copy in loads:
        copy.start()

    dp, x, core = position()
    yz = dp // 2
    y = yz % Y
    z = yz // Y
    me = x * nyz + yz
    zs = [(z + d) % Z for d in range(Z)]
    ys = [(y + d) % Y for d in range(Y)]
    partner = (yz * 2 + 1 - core, x)

    def at(dz, dy, dx=0):
        return ((zs[dz % Z] * Y + ys[dy % Y]) * 2 + core, (x + dx) % X)

    def signal(sem, where):
        pl.semaphore_signal(sem, inc=1, device_id=where, device_id_type=MESH)

    def start(src, dst, send_sem, recv_sem, where):
        pltpu.make_async_remote_copy(
            src_ref=src, dst_ref=dst, send_sem=send_sem, recv_sem=recv_sem,
            device_id=where, device_id_type=MESH,
        ).start()

    barrier = pltpu.get_barrier_semaphore()
    for d in range(1, Z):
        signal(barrier, at(d, 0))
    for d in range(1, Y):
        signal(barrier, at(0, d))
    for d in range(1, X):
        signal(barrier, at(0, 0, d))
    signal(barrier, partner)

    loads[0].wait()
    lrow = lab[...]
    rank = ranks(lrow)
    lx, lyz = lrow // nyz, lrow % nyz
    code = ((lyz // Y + Z - z) % Z) * Y + (lyz % Y + Y - y) % Y
    target = 2 * (((code * back) % nyz) * X + (lx + X - x) % X) + rank

    pl.semaphore_wait(barrier, Z + Y + X - 2)
    for d in range(1, Y):
        signal(line_sem, at(0, d))

    for copy in loads[1:]:
        copy.wait()
    e = emb[...]
    unit = e * lax.rsqrt(jnp.sum(e * e, axis=1, keepdims=True) + epsilon)
    parts = split3(unit)

    n_chunk = min(4, n_group)
    chunk = own // n_chunk
    chunk_q = nyz // n_chunk

    def fill(i):
        low = i * chunk
        place = jnp.where(iota((chunk, rows), 0) + low == target, 1.0, 0.0)
        filled = jnp.sum(place, axis=1, keepdims=True) > 0.5
        place = place.astype(bf16)
        slots = sum(jnp.dot(place, p, preferred_element_type=f32) for p in parts)
        slots = jnp.where(filled, slots, SENTINEL)
        for t in range(tiles):
            send[pl.ds(low * tiles + t, chunk, stride=tiles), :] = (
                slots[:, t * 128:(t + 1) * 128])

    def straight(q, dx):
        w = (q * STRIDE) % nyz
        where = (((z + w // Y) % Z * Y + (y + w % Y) % Y) * 2 + core, (x + dx) % X)
        piece = pl.ds((q * X + dx) * msg, msg)
        start(send.at[piece], recv.at[piece], fs, fr.at[q // GROUP], where)

    def straight_all(first, last, dxs):
        def step(q, carry):
            for dx in dxs:
                straight(q, dx)
            return carry
        lax.fori_loop(first, last, step, 0)

    fill(0)
    pl.semaphore_wait(line_sem, Y - 1)
    for d in range(1, X):
        signal(plane_sem, at(0, 0, d))
    straight_all(1, chunk_q, [0])
    recv[0:msg, :] = send[0:msg, :]
    fill(1)
    pl.semaphore_wait(plane_sem, X - 1)
    straight_all(0, chunk_q, range(1, X))
    for i in range(1, n_chunk):
        if i > 1:
            fill(i)
        straight_all(i * chunk_q, (i + 1) * chunk_q, range(X))

    grows = GROUP * X * msg
    krows = GROUP * X * 2

    def take(buf, g, base, total):
        columns = []
        dead = None
        for t in range(tiles):
            pieces = []
            for dx in range(X):
                for s in range(2):
                    first = g * grows + dx * msg + s * tiles + t
                    pieces.append(buf[pl.ds(first, GROUP, stride=X * msg), :])
            v = jnp.concatenate(pieces, axis=0)
            if dead is None:
                dead = v > 2.0
                bias[pl.ds(base + g * krows, krows), :] = jnp.where(dead, -4.0, 0.0)
            v = jnp.where(dead, 0.0, v)
            hi = v.astype(bf16)
            lo = (v - hi.astype(f32)).astype(bf16)
            for i, v_part in enumerate((hi, lo, hi)):
                keys[pl.ds(base + g * krows, krows), pl.ds(i * width + t * 128, 128)] = v_part
            columns.append(jnp.sum(v, axis=0, keepdims=True))
        return total + jnp.concatenate(columns, axis=1)

    half = own // 2

    def product(first, count, side):
        return jnp.dot(keys[first:first + count, :], queries[:, side * half:(side + 1) * half],
                       preferred_element_type=f32)

    def closest(s, first, side):
        count = s.shape[0]
        off = bias[first:first + count, :]
        s = s + (jnp.concatenate([off] * (half // 128), axis=1) if half > 128 else off[:, :half])
        if first < own:
            itself = iota((count, half), 0) + first == iota((count, half), 1) + side * half
            s = jnp.where(itself, -4.0, s)
        return jnp.max(s, axis=0, keepdims=True)

    best = [jnp.full((1, half), -1.0, f32)] * 2

    def compare(first, count, side):
        best[side] = jnp.maximum(best[side], closest(product(first, count, side), first, side))

    mine = jnp.zeros((1, width), f32)
    for g in range(n_group):
        missing = msg if g == 0 else 0
        wait_rows(recv, g * grows + missing, grows - missing, fr.at[g])
        piece = pl.ds(g * grows, grows)
        start(recv.at[piece], other.at[piece], ps, pr.at[g], partner)
        mine = take(recv, g, 0, mine)
        have = (g + 1) * krows
        turn = 128 if half % 128 == 0 else krows
        if have % turn == 0:
            top = pl.ds(have - turn, turn)
            for t in range(tiles):
                hi = keys[top, pl.ds(t * 128, 128)].astype(f32).T.astype(bf16)
                lo = keys[top, pl.ds(width + t * 128, 128)].astype(f32).T.astype(bf16)
                for i, v_part in enumerate((hi, hi, lo)):
                    queries[pl.ds(i * width + t * 128, 128), top] = v_part
        if g == n_group - 1:
            part_sum[0] = mine
            start(part_sum.at[0], part_sum.at[1], ss, sr, partner)
            break
        wait_rows(other, g * grows, grows, pr.at[g])
        take(other, g, own, mine)
        if have == half:
            seen = 0
        if have == half or (have > half and (have - half) % 128 == 0):
            compare(seen, have - seen, 0)
            compare(own + seen, have - seen, 0)
            seen = have

    wait_rows(part_sum, 1, 1, sr)
    sums = mine + part_sum[1]
    fresh = sums * lax.rsqrt(jnp.sum(sums * sums, axis=1, keepdims=True) + epsilon)
    for t in range(half_t):
        a = fresh[:, t * 128:(t + 1) * 128]
        b = fresh[:, (half_t + t) * 128:(half_t + t + 1) * 128]
        frow[pl.ds(me * half_t + t, 1), :] = jnp.where(core == 0, a, b)
    piece = pl.ds(me * half_t, half_t)
    for d in range(1, Y):
        start(frow.at[piece], frow.at[piece], nys, nyr, at(0, d))
    fh = fresh.astype(bf16)
    fl = jnp.broadcast_to(fresh - fh.astype(f32), (16, width)).astype(bf16)
    fh = jnp.broadcast_to(fresh, (16, width)).astype(bf16)
    keys[2 * own:2 * own + 16, :] = jnp.concatenate([fh, fl, fh], axis=1)

    xrows = nyz * half_t
    hrows = xrows // 2

    def block_of(dx, half):
        return pl.ds(((x + dx) % X) * xrows + half * hrows, hrows)

    def along(dx, half, sem, to):
        piece = block_of(dx, half)
        start(frow.at[piece], frow.at[piece], nxs, nxr.at[sem], at(0, 0, to))

    def pass_on(dx):
        piece = pl.ds(((x + dx) % X) * xrows, xrows)
        start(frow.at[piece], fpart.at[piece], ncs, ncr.at[dx], partner)

    def landed(dx, half, sem):
        wait_rows(frow, ((x + dx) % X) * xrows + half * hrows, hrows, nxr.at[sem])

    wait_rows(other, (n_group - 1) * grows, grows, pr.at[n_group - 1])
    take(other, n_group - 1, own, mine)
    compare(0, half, 1)
    compare(half, half, 1)

    yrows = Y * half_t
    wait_rows(frow, 0, (Y - 1) * half_t, nyr)
    piece = pl.ds((x * nyz + z * Y) * half_t, yrows)
    for d in range(1, Z):
        start(frow.at[piece], frow.at[piece], nzs, nzr, at(d, 0))

    compare(seen, own - seen, 0)
    compare(own, half, 1)

    wait_rows(frow, 0, (Z - 1) * yrows, nzr)
    along(0, 0, 0, 1)
    if X > 2:
        along(0, 1, 2, X - 1)
    along(0, 1, 1, 1)
    if X > 2:
        along(0, 0, 3, X - 1)
    pass_on(0)

    cos = []
    for side, first in ((0, own + seen), (1, own + half)):
        count = 2 * own - first
        s = product(first, count + 16, side)
        best[side] = jnp.maximum(best[side], closest(s[:count, :], first, side))
        cos.append(s[count:count + 1, :])
    best = jnp.concatenate(best, axis=1)
    cos = jnp.concatenate(cos, axis=1)

    xs = (iota((128, own), 1) // GROUP) % (2 * X)
    lane_of = (xs // 2) * 8 + (xs % 2) * 2
    j = iota((128, own), 0)
    spread = jnp.where(j == lane_of, best, jnp.where(j == lane_of + 1, cos, 0.0))
    spread = spread.T.reshape(n_group, 2 * X, GROUP, 128)
    spread = jnp.sum(spread, axis=1).reshape(nyz, 128)
    for q in range(nyz):
        dz, dy = (q * STRIDE) % nyz // Y, (q * STRIDE) % nyz % Y
        abuf[dy * Z + dz:dy * Z + dz + 1, :] = spread[q:q + 1, :]
    for d in range(1, Y):
        start(abuf.at[pl.ds(d * Z, Z)], ay.at[pl.ds(y * Z, Z)], ays, ayr, at(0, -d))
    ay[pl.ds(y * Z, Z), :] = abuf[0:Z, :]

    if X > 2:
        landed(X - 1, 0, 0)
        along(X - 1, 0, 4, 1)
        landed(1, 1, 2)
        along(1, 1, 5, X - 1)

    wait_rows(ay, 0, (Y - 1) * Z, ayr)
    for dz in range(Z):
        ab[dz * Y:(dz + 1) * Y, :] = ay[pl.ds(dz, Y, stride=Z), :]
    for d in range(1, Z):
        start(ab.at[pl.ds(d * Y, Y)], az.at[pl.ds(z * Y, Y)], azs, azr, at(-d, 0))
    az[pl.ds(z * Y, Y), :] = ab[0:Y, :]

    if X > 2:
        landed(X - 1, 1, 1)
        pass_on(X - 1)
        landed(1, 0, 3)
        pass_on(1)
    else:
        landed(1, 0, 0)
        landed(1, 1, 1)
        pass_on(1)

    wait_rows(az, 0, (Z - 1) * Y, azr)
    wait_rows(ay, 0, (Y - 1) * Z, ays)
    turned = jnp.concatenate([az[...], jnp.zeros((128 - nyz, 128), f32)], axis=0).T
    abuf[0:8 * X, :] = turned[0:8 * X, :]
    for d in range(1, X):
        start(abuf.at[pl.ds(d * 8, 8)], ans.at[pl.ds(x * 8, 8)], axs, axr, at(0, 0, X - d))
    ans[pl.ds(x * 8, 8), :] = abuf[0:8, :]

    if X > 2:
        landed(2, 0, 4)
        landed(2, 1, 5)
        pass_on(2)
    for dx in range(X):
        wait_rows(fpart, ((x + dx) % X) * xrows, xrows, ncr.at[dx])
    wait_rows(ans, 0, (X - 1) * 8, axr)

    wait_rows(send, 0, (chips - 1) * msg, fs)
    wait_rows(part_sum, 0, 1, ss)
    wait_rows(recv, 0, n_group * grows, ps)
    wait_rows(frow, 0, (Y - 1) * half_t, nys)
    wait_rows(frow, 0, (Z - 1) * yrows, nzs)
    wait_rows(frow, 0, (X - 1) * xrows, nxs)
    wait_rows(frow, 0, X * xrows, ncs)
    wait_rows(az, 0, (Z - 1) * Y, azs)
    wait_rows(ans, 0, (X - 1) * 8, axs)


def finish(dims, frow, fpart, ans, lab, slab, cent, table_hbm, cos_hbm, sim_hbm,
           table, cos_out, sim_out, put):
    Z, Y, X = dims
    nyz = Z * Y
    chips = nyz * X
    trows, width = cent.shape
    half_t = width // 256
    dp, x, core = position()
    rows = lab.shape[1]

    low, high = [], []
    for t in range(half_t):
        a = frow[pl.ds(t, chips, stride=half_t), :]
        b = fpart[pl.ds(t, chips, stride=half_t), :]
        low.append(jnp.where(core == 0, a, b))
        high.append(jnp.where(core == 0, b, a))
    full = jnp.concatenate(low + high, axis=1)
    row_id = (dp * X + x) * trows + iota((trows, chips), 0)
    hit = jnp.where(row_id == slab[...], 1.0, 0.0)
    named = jnp.sum(hit, axis=1, keepdims=True) > 0.5
    table[...] = jnp.where(named, select_rows(hit.astype(bf16), full), cent[...])
    pairs = [(cos_out, cos_hbm), (sim_out, sim_hbm)]
    part = trows // 4
    pairs += [
        (table.at[pl.ds(i * part, part)], table_hbm.at[pl.ds(i * part, part)]) for i in range(4)]
    puts = [pltpu.make_async_copy(src, dst, put.at[i]) for i, (src, dst) in enumerate(pairs)]
    for copy in puts[2:]:
        copy.start()

    lrow = lab[...]
    rank = ranks(lrow)
    spot = (lrow // nyz) * 128 + lrow % nyz
    member = jnp.where(iota((X * 128, rows), 0) == spot, 1.0, 0.0).astype(bf16)
    got = jnp.concatenate([ans[i * 8:(i + 1) * 8, :] for i in range(X)], axis=1)
    got = jnp.concatenate([got, jnp.zeros_like(got)], axis=0)
    got = sum(jnp.dot(p, member, preferred_element_type=f32) for p in split3(got))
    sim_out[...] = jnp.where(rank == 0, got[0:1, :], got[2:3, :])
    cos_out[...] = jnp.where(rank == 0, got[1:2, :], got[3:4, :])
    puts[0].start()
    puts[1].start()
    for copy in puts:
        copy.wait()


def local(dims, embeddings, assignment, slab_ids, centroids):
    Z, Y, X = dims
    nyz = Z * Y
    chips = nyz * X
    rows, width = embeddings.shape
    tiles = width // 128
    n_group = nyz // GROUP
    linear = 2 * chips * tiles
    half = chips * tiles // 2
    dma = pltpu.SemaphoreType.DMA
    vmem = pl.BlockSpec(memory_space=pltpu.VMEM)
    hbm = pl.BlockSpec(memory_space=pl.ANY)
    shape = jax.ShapeDtypeStruct
    regular = pltpu.SemaphoreType.REGULAR
    labels = assignment.reshape(1, rows)
    slabs = slab_ids.reshape(1, chips)

    given = pl.pallas_call(
        functools.partial(exchange, dims),
        out_shape=(
            shape((half, 128), f32),
            shape((half, 128), f32),
            shape((8 * X, 128), f32),
        ),
        in_specs=[hbm] * 2 + [vmem],
        out_specs=(vmem,) * 3,
        scratch_shapes=[
            pltpu.VMEM((rows, width), f32),
            pltpu.VMEM((1, rows), jnp.int32),
            pltpu.VMEM((linear, 128), f32),
            pltpu.VMEM((linear, 128), f32),
            pltpu.VMEM((linear, 128), f32),
            pltpu.VMEM((4 * chips + 16, 3 * width), bf16),
            pltpu.VMEM((3 * width, 2 * chips), bf16),
            pltpu.VMEM((4 * chips, 128), f32),
            pltpu.VMEM((2, 1, width), f32),
            pltpu.VMEM((max(nyz, 8 * X), 128), f32),
            pltpu.VMEM((nyz, 128), f32),
            pltpu.VMEM((nyz, 128), f32),
            pltpu.VMEM((nyz, 128), f32),
            regular, regular,
            dma((5,)),
            dma, dma((n_group,)), dma, dma((n_group,)), dma, dma,
            dma, dma, dma, dma, dma, dma((6,)), dma, dma((X,)),
            dma, dma, dma, dma, dma, dma,
        ],
        compiler_params=pltpu.CompilerParams(
            collective_id=0, has_side_effects=True, vmem_limit_bytes=KERNEL_BYTES),
    )(embeddings, labels, slabs)

    table, cos, sim = pl.pallas_call(
        functools.partial(finish, dims),
        out_shape=(
            shape(centroids.shape, f32),
            shape((1, rows), f32),
            shape((1, rows), f32),
        ),
        in_specs=[vmem] * 6,
        out_specs=(hbm,) * 3,
        scratch_shapes=[
            pltpu.VMEM(centroids.shape, f32),
            pltpu.VMEM((1, rows), f32),
            pltpu.VMEM((1, rows), f32),
            dma((6,)),
        ],
        compiler_params=pltpu.CompilerParams(vmem_limit_bytes=32 * 2**20),
    )(*given, labels, slabs, centroids)
    return table, cos.reshape(rows), sim.reshape(rows)


def solution(mesh, dims=(Z, Y, X)):
    placed = (P(("dp", "cent"), None), P(("dp", "cent"), None), P(), P(("dp", "cent"), None))
    return jax.shard_map(
        functools.partial(local, dims),
        mesh=mesh,
        in_specs=placed,
        out_specs=(P(("dp", "cent"), None), P(("dp", "cent")), P(("dp", "cent"))),
        check_vma=False,
    )
```

```python
import functools

import jax
import jax.numpy as jnp
from jax import lax
from jax.experimental import pallas as pl
from jax.experimental.pallas import tpu as pltpu
from jax.sharding import PartitionSpec as P

epsilon = 1e-06
Z, Y, X = 8, 8, 4
GROUP = 8
KERNEL_BYTES = 105 * 2**19
SENTINEL = 4.0
STRIDE = 37
MESH = pl.DeviceIdType.MESH
f32, bf16 = jnp.float32, jnp.bfloat16


def split3(v):
    hi = v.astype(bf16)
    rest = v - hi.astype(f32)
    mid = rest.astype(bf16)
    lo = (rest - mid.astype(f32)).astype(bf16)
    return hi, mid, lo


def select_rows(onehot, v):
    hi, mid, lo = split3(v)
    dot = functools.partial(jnp.dot, preferred_element_type=f32)
    return dot(onehot, hi) + dot(onehot, mid) + dot(onehot, lo)


def iota(shape, axis):
    return lax.broadcasted_iota(jnp.int32, shape, axis)


def position():
    dp = lax.axis_index("dp")
    return dp, lax.axis_index("cent"), dp % 2


def wait_rows(buf, start, count, sem):
    part = buf.at[pl.ds(start, count)]
    pltpu.make_async_copy(part, part, sem).wait()


def ranks(lrow):
    rows = lrow.shape[1]
    lcol = jnp.broadcast_to(lrow.astype(f32), (128, rows)).T[:, 0:1].astype(jnp.int32)
    earlier = (lcol == lrow) & (iota((rows, rows), 0) < iota((rows, rows), 1))
    return jnp.sum(jnp.where(earlier, 1.0, 0.0), axis=0, keepdims=True).astype(jnp.int32)


def exchange(dims, emb_hbm, lab_hbm, slab, frow, fpart, ans,
             emb, lab, send, recv, other, khi, klo, qht, qlt, bias, part_sum,
             abuf, ay, ab, az,
             line_sem, plane_sem, load, fs, fr, ps, pr, ss, sr,
             nys, nyr, nzs, nzr, nxs, nxr, ncs, ncr, ays, ayr, azs, azr, axs, axr):
    Z, Y, X = dims
    nyz = Z * Y
    chips = nyz * X
    n_group = nyz // GROUP
    rows, width = emb.shape
    tiles = width // 128
    half_t = tiles // 2
    msg = 2 * tiles
    own = 2 * chips
    back = pow(STRIDE, -1, nyz)

    loads = [pltpu.make_async_copy(lab_hbm, lab, load.at[0])]
    part = rows // 4
    loads += [
        pltpu.make_async_copy(
            emb_hbm.at[pl.ds(i * part, part)], emb.at[pl.ds(i * part, part)], load.at[1 + i])
        for i in range(4)
    ]
    for copy in loads:
        copy.start()

    dp, x, core = position()
    yz = dp // 2
    y = yz % Y
    z = yz // Y
    me = x * nyz + yz
    zs = [(z + d) % Z for d in range(Z)]
    ys = [(y + d) % Y for d in range(Y)]
    partner = (yz * 2 + 1 - core, x)

    def at(dz, dy, dx=0):
        return ((zs[dz % Z] * Y + ys[dy % Y]) * 2 + core, (x + dx) % X)

    def signal(sem, where):
        pl.semaphore_signal(sem, inc=1, device_id=where, device_id_type=MESH)

    def start(src, dst, send_sem, recv_sem, where):
        pltpu.make_async_remote_copy(
            src_ref=src, dst_ref=dst, send_sem=send_sem, recv_sem=recv_sem,
            device_id=where, device_id_type=MESH,
        ).start()

    barrier = pltpu.get_barrier_semaphore()
    for d in range(1, Z):
        signal(barrier, at(d, 0))
    for d in range(1, Y):
        signal(barrier, at(0, d))
    for d in range(1, X):
        signal(barrier, at(0, 0, d))
    signal(barrier, partner)

    loads[0].wait()
    lrow = lab[...]
    rank = ranks(lrow)
    lx, lyz = lrow // nyz, lrow % nyz
    code = ((lyz // Y + Z - z) % Z) * Y + (lyz % Y + Y - y) % Y
    target = 2 * (((code * back) % nyz) * X + (lx + X - x) % X) + rank

    pl.semaphore_wait(barrier, Z + Y + X - 2)
    for d in range(1, Y):
        signal(line_sem, at(0, d))

    for copy in loads[1:]:
        copy.wait()
    e = emb[...]
    unit = e * lax.rsqrt(jnp.sum(e * e, axis=1, keepdims=True) + epsilon)
    parts = split3(unit)

    n_chunk = min(4, n_group)
    chunk = own // n_chunk
    chunk_q = nyz // n_chunk

    def fill(i):
        low = i * chunk
        place = jnp.where(iota((chunk, rows), 0) + low == target, 1.0, 0.0)
        filled = jnp.sum(place, axis=1, keepdims=True) > 0.5
        place = place.astype(bf16)
        slots = sum(jnp.dot(place, p, preferred_element_type=f32) for p in parts)
        slots = jnp.where(filled, slots, SENTINEL)
        for t in range(tiles):
            send[pl.ds(low * tiles + t, chunk, stride=tiles), :] = (
                slots[:, t * 128:(t + 1) * 128])

    def straight(q, dx):
        w = (q * STRIDE) % nyz
        where = (((z + w // Y) % Z * Y + (y + w % Y) % Y) * 2 + core, (x + dx) % X)
        piece = pl.ds((q * X + dx) * msg, msg)
        start(send.at[piece], recv.at[piece], fs, fr.at[q // GROUP], where)

    def straight_all(first, last, dxs):
        def step(q, carry):
            for dx in dxs:
                straight(q, dx)
            return carry
        lax.fori_loop(first, last, step, 0)

    fill(0)
    pl.semaphore_wait(line_sem, Y - 1)
    for d in range(1, X):
        signal(plane_sem, at(0, 0, d))
    straight_all(1, chunk_q, [0])
    recv[0:msg, :] = send[0:msg, :]
    fill(1)
    pl.semaphore_wait(plane_sem, X - 1)
    straight_all(0, chunk_q, range(1, X))
    for i in range(1, n_chunk):
        if i > 1:
            fill(i)
        straight_all(i * chunk_q, (i + 1) * chunk_q, range(X))

    grows = GROUP * X * msg
    krows = GROUP * X * 2

    def take(buf, g, base, total):
        columns = []
        dead = None
        for t in range(tiles):
            v = buf[pl.ds(g * grows + t, krows, stride=tiles), :]
            if dead is None:
                dead = v > 2.0
                bias[pl.ds(base + g * krows, krows), :] = jnp.where(dead, -4.0, 0.0)
            v = jnp.where(dead, 0.0, v)
            hi = v.astype(bf16)
            lo = (v - hi.astype(f32)).astype(bf16)
            khi[pl.ds(base + g * krows, krows), t * 128:(t + 1) * 128] = hi
            klo[pl.ds(base + g * krows, krows), t * 128:(t + 1) * 128] = lo
            columns.append(jnp.sum(v, axis=0, keepdims=True))
        return total + jnp.concatenate(columns, axis=1)

    def take_own(g, total):
        total = take(recv, g, 0, total)
        have = (g + 1) * krows
        turn = 128 if own % 128 == 0 else krows
        if have % turn == 0:
            top = pl.ds(have - turn, turn)
            for t in range(tiles):
                lanes = pl.ds(t * 128, 128)
                qht[lanes, top] = khi[top, lanes].astype(f32).T.astype(bf16)
                qlt[lanes, top] = klo[top, lanes].astype(f32).T.astype(bf16)
        return total

    def take_other(g):
        wait_rows(other, g * grows, grows, pr.at[g])
        take(other, g, own, mine)

    mine = jnp.zeros((1, width), f32)
    for g in range(n_group):
        missing = msg if g == 0 else 0
        wait_rows(recv, g * grows + missing, grows - missing, fr.at[g])
        piece = pl.ds(g * grows, grows)
        start(recv.at[piece], other.at[piece], ps, pr.at[g], partner)
        if g > 0:
            mine = take_own(g - 1, mine)
        if g > 1:
            take_other(g - 2)
    mine = take_own(n_group - 1, mine)
    part_sum[0] = mine
    start(part_sum.at[0], part_sum.at[1], ss, sr, partner)
    for g in range(max(n_group - 2, 0), n_group):
        take_other(g)

    wait_rows(part_sum, 1, 1, sr)
    sums = mine + part_sum[1]
    fresh = sums * lax.rsqrt(jnp.sum(sums * sums, axis=1, keepdims=True) + epsilon)
    for t in range(half_t):
        a = fresh[:, t * 128:(t + 1) * 128]
        b = fresh[:, (half_t + t) * 128:(half_t + t + 1) * 128]
        frow[pl.ds(me * half_t + t, 1), :] = jnp.where(core == 0, a, b)
    piece = pl.ds(me * half_t, half_t)
    for d in range(1, Y):
        start(frow.at[piece], frow.at[piece], nys, nyr, at(0, d))
    fh = fresh.astype(bf16)
    khi[2 * own:2 * own + 16, :] = jnp.broadcast_to(fresh, (16, width)).astype(bf16)
    klo[2 * own:2 * own + 16, :] = jnp.broadcast_to(
        fresh - fh.astype(f32), (16, width)).astype(bf16)

    def product(first, count):
        kh = khi[first:first + count, :]
        kl = klo[first:first + count, :]
        dot = functools.partial(jnp.dot, preferred_element_type=f32)
        return dot(kh, qht[...]) + dot(kh, qlt[...]) + dot(kl, qht[...])

    def closest(s, first):
        off = bias[first:first + own, :]
        s = s + (jnp.concatenate([off] * (own // 128), axis=1) if own > 128 else off[:, :own])
        if first == 0:
            s = jnp.where(iota((own, own), 0) == iota((own, own), 1), -4.0, s)
        return jnp.max(s, axis=0, keepdims=True)

    best = jnp.maximum(closest(product(0, own), 0), -1.0)

    yrows = Y * half_t
    wait_rows(frow, 0, (Y - 1) * half_t, nyr)
    piece = pl.ds((x * nyz + z * Y) * half_t, yrows)
    for d in range(1, Z):
        start(frow.at[piece], frow.at[piece], nzs, nzr, at(d, 0))

    s = product(own, own + 16)
    best = jnp.maximum(best, closest(s[:own, :], own))
    cos = s[own:own + 1, :]

    xs = iota((128, own), 1) % (2 * X)
    lane_of = (xs // 2) * 8 + (xs % 2) * 2
    j = iota((128, own), 0)
    spread = jnp.where(j == lane_of, best, jnp.where(j == lane_of + 1, cos, 0.0))
    spread = jnp.sum(spread.T.reshape(nyz, 2 * X, 128), axis=1)
    for q in range(nyz):
        dz, dy = (q * STRIDE) % nyz // Y, (q * STRIDE) % nyz % Y
        abuf[dy * Z + dz:dy * Z + dz + 1, :] = spread[q:q + 1, :]
    for d in range(1, Y):
        start(abuf.at[pl.ds(d * Z, Z)], ay.at[pl.ds(y * Z, Z)], ays, ayr, at(0, -d))
    ay[pl.ds(y * Z, Z), :] = abuf[0:Z, :]

    xrows = nyz * half_t
    hrows = xrows // 2

    def block_of(dx, half):
        return pl.ds(((x + dx) % X) * xrows + half * hrows, hrows)

    def along(dx, half, sem, to):
        piece = block_of(dx, half)
        start(frow.at[piece], frow.at[piece], nxs, nxr.at[sem], at(0, 0, to))

    def pass_on(dx):
        piece = pl.ds(((x + dx) % X) * xrows, xrows)
        start(frow.at[piece], fpart.at[piece], ncs, ncr.at[dx], partner)

    def landed(dx, half, sem):
        wait_rows(frow, ((x + dx) % X) * xrows + half * hrows, hrows, nxr.at[sem])

    wait_rows(frow, 0, (Z - 1) * yrows, nzr)
    along(0, 0, 0, 1)
    if X > 2:
        along(0, 1, 2, X - 1)
    along(0, 1, 1, 1)
    if X > 2:
        along(0, 0, 3, X - 1)
    pass_on(0)
    if X > 2:
        landed(X - 1, 0, 0)
        along(X - 1, 0, 4, 1)
        landed(1, 1, 2)
        along(1, 1, 5, X - 1)

    wait_rows(ay, 0, (Y - 1) * Z, ayr)
    for dz in range(Z):
        ab[dz * Y:(dz + 1) * Y, :] = ay[pl.ds(dz, Y, stride=Z), :]
    for d in range(1, Z):
        start(ab.at[pl.ds(d * Y, Y)], az.at[pl.ds(z * Y, Y)], azs, azr, at(-d, 0))
    az[pl.ds(z * Y, Y), :] = ab[0:Y, :]

    if X > 2:
        landed(X - 1, 1, 1)
        pass_on(X - 1)
        landed(1, 0, 3)
        pass_on(1)
    else:
        landed(1, 0, 0)
        landed(1, 1, 1)
        pass_on(1)

    wait_rows(az, 0, (Z - 1) * Y, azr)
    wait_rows(ay, 0, (Y - 1) * Z, ays)
    turned = jnp.concatenate([az[...], jnp.zeros((128 - nyz, 128), f32)], axis=0).T
    abuf[0:8 * X, :] = turned[0:8 * X, :]
    for d in range(1, X):
        start(abuf.at[pl.ds(d * 8, 8)], ans.at[pl.ds(x * 8, 8)], axs, axr, at(0, 0, X - d))
    ans[pl.ds(x * 8, 8), :] = abuf[0:8, :]

    if X > 2:
        landed(2, 0, 4)
        landed(2, 1, 5)
        pass_on(2)
    for dx in range(X):
        wait_rows(fpart, ((x + dx) % X) * xrows, xrows, ncr.at[dx])
    wait_rows(ans, 0, (X - 1) * 8, axr)

    wait_rows(send, 0, (chips - 1) * msg, fs)
    wait_rows(part_sum, 0, 1, ss)
    wait_rows(recv, 0, n_group * grows, ps)
    wait_rows(frow, 0, (Y - 1) * half_t, nys)
    wait_rows(frow, 0, (Z - 1) * yrows, nzs)
    wait_rows(frow, 0, (X - 1) * xrows, nxs)
    wait_rows(frow, 0, X * xrows, ncs)
    wait_rows(az, 0, (Z - 1) * Y, azs)
    wait_rows(ans, 0, (X - 1) * 8, axs)


def finish(dims, frow, fpart, ans, lab, slab, cent, table_hbm, cos_hbm, sim_hbm,
           table, cos_out, sim_out, put):
    Z, Y, X = dims
    nyz = Z * Y
    chips = nyz * X
    trows, width = cent.shape
    half_t = width // 256
    dp, x, core = position()
    rows = lab.shape[1]

    low, high = [], []
    for t in range(half_t):
        a = frow[pl.ds(t, chips, stride=half_t), :]
        b = fpart[pl.ds(t, chips, stride=half_t), :]
        low.append(jnp.where(core == 0, a, b))
        high.append(jnp.where(core == 0, b, a))
    full = jnp.concatenate(low + high, axis=1)
    row_id = (dp * X + x) * trows + iota((trows, chips), 0)
    hit = jnp.where(row_id == slab[...], 1.0, 0.0)
    named = jnp.sum(hit, axis=1, keepdims=True) > 0.5
    table[...] = jnp.where(named, select_rows(hit.astype(bf16), full), cent[...])
    pairs = [(cos_out, cos_hbm), (sim_out, sim_hbm)]
    part = trows // 4
    pairs += [
        (table.at[pl.ds(i * part, part)], table_hbm.at[pl.ds(i * part, part)]) for i in range(4)]
    puts = [pltpu.make_async_copy(src, dst, put.at[i]) for i, (src, dst) in enumerate(pairs)]
    for copy in puts[2:]:
        copy.start()

    lrow = lab[...]
    rank = ranks(lrow)
    spot = (lrow // nyz) * 128 + lrow % nyz
    member = jnp.where(iota((X * 128, rows), 0) == spot, 1.0, 0.0).astype(bf16)
    got = jnp.concatenate([ans[i * 8:(i + 1) * 8, :] for i in range(X)], axis=1)
    got = jnp.concatenate([got, jnp.zeros_like(got)], axis=0)
    got = sum(jnp.dot(p, member, preferred_element_type=f32) for p in split3(got))
    sim_out[...] = jnp.where(rank == 0, got[0:1, :], got[2:3, :])
    cos_out[...] = jnp.where(rank == 0, got[1:2, :], got[3:4, :])
    puts[0].start()
    puts[1].start()
    for copy in puts:
        copy.wait()


def local(dims, embeddings, assignment, slab_ids, centroids):
    Z, Y, X = dims
    nyz = Z * Y
    chips = nyz * X
    rows, width = embeddings.shape
    tiles = width // 128
    n_group = nyz // GROUP
    linear = 2 * chips * tiles
    half = chips * tiles // 2
    dma = pltpu.SemaphoreType.DMA
    vmem = pl.BlockSpec(memory_space=pltpu.VMEM)
    hbm = pl.BlockSpec(memory_space=pl.ANY)
    shape = jax.ShapeDtypeStruct
    regular = pltpu.SemaphoreType.REGULAR
    labels = assignment.reshape(1, rows)
    slabs = slab_ids.reshape(1, chips)

    given = pl.pallas_call(
        functools.partial(exchange, dims),
        out_shape=(
            shape((half, 128), f32),
            shape((half, 128), f32),
            shape((8 * X, 128), f32),
        ),
        in_specs=[hbm] * 2 + [vmem],
        out_specs=(vmem,) * 3,
        scratch_shapes=[
            pltpu.VMEM((rows, width), f32),
            pltpu.VMEM((1, rows), jnp.int32),
            pltpu.VMEM((linear, 128), f32),
            pltpu.VMEM((linear, 128), f32),
            pltpu.VMEM((linear, 128), f32),
            pltpu.VMEM((4 * chips + 16, width), bf16),
            pltpu.VMEM((4 * chips + 16, width), bf16),
            pltpu.VMEM((width, 2 * chips), bf16),
            pltpu.VMEM((width, 2 * chips), bf16),
            pltpu.VMEM((4 * chips, 128), f32),
            pltpu.VMEM((2, 1, width), f32),
            pltpu.VMEM((max(nyz, 8 * X), 128), f32),
            pltpu.VMEM((nyz, 128), f32),
            pltpu.VMEM((nyz, 128), f32),
            pltpu.VMEM((nyz, 128), f32),
            regular, regular,
            dma((5,)),
            dma, dma((n_group,)), dma, dma((n_group,)), dma, dma,
            dma, dma, dma, dma, dma, dma((6,)), dma, dma((X,)),
            dma, dma, dma, dma, dma, dma,
        ],
        compiler_params=pltpu.CompilerParams(
            collective_id=0, has_side_effects=True, vmem_limit_bytes=KERNEL_BYTES),
    )(embeddings, labels, slabs)

    table, cos, sim = pl.pallas_call(
        functools.partial(finish, dims),
        out_shape=(
            shape(centroids.shape, f32),
            shape((1, rows), f32),
            shape((1, rows), f32),
        ),
        in_specs=[vmem] * 6,
        out_specs=(hbm,) * 3,
        scratch_shapes=[
            pltpu.VMEM(centroids.shape, f32),
            pltpu.VMEM((1, rows), f32),
            pltpu.VMEM((1, rows), f32),
            dma((6,)),
        ],
        compiler_params=pltpu.CompilerParams(vmem_limit_bytes=32 * 2**20),
    )(*given, labels, slabs, centroids)
    return table, cos.reshape(rows), sim.reshape(rows)


def solution(mesh, dims=(Z, Y, X)):
    placed = (P(("dp", "cent"), None), P(("dp", "cent"), None), P(), P(("dp", "cent"), None))
    return jax.shard_map(
        functools.partial(local, dims),
        mesh=mesh,
        in_specs=placed,
        out_specs=(P(("dp", "cent"), None), P(("dp", "cent")), P(("dp", "cent"))),
        check_vma=False,
    )
```

```python
import functools

import jax
import jax.numpy as jnp
from jax import lax
from jax.experimental import pallas as pl
from jax.experimental.pallas import tpu as pltpu
from jax.sharding import PartitionSpec as P

epsilon = 1e-06
Z, Y, X = 8, 8, 4
GROUP = 8
KERNEL_BYTES = 105 * 2**19
SENTINEL = 4.0
STRIDE = 37
MESH = pl.DeviceIdType.MESH
f32, bf16 = jnp.float32, jnp.bfloat16


def split3(v):
    hi = v.astype(bf16)
    rest = v - hi.astype(f32)
    mid = rest.astype(bf16)
    lo = (rest - mid.astype(f32)).astype(bf16)
    return hi, mid, lo


def select_rows(onehot, v):
    hi, mid, lo = split3(v)
    dot = functools.partial(jnp.dot, preferred_element_type=f32)
    return dot(onehot, hi) + dot(onehot, mid) + dot(onehot, lo)


def iota(shape, axis):
    return lax.broadcasted_iota(jnp.int32, shape, axis)


def position():
    dp = lax.axis_index("dp")
    return dp, lax.axis_index("cent"), dp % 2


def wait_rows(buf, start, count, sem):
    part = buf.at[pl.ds(start, count)]
    pltpu.make_async_copy(part, part, sem).wait()


def ranks(lrow):
    rows = lrow.shape[1]
    lcol = jnp.broadcast_to(lrow.astype(f32), (128, rows)).T[:, 0:1].astype(jnp.int32)
    earlier = (lcol == lrow) & (iota((rows, rows), 0) < iota((rows, rows), 1))
    return jnp.sum(jnp.where(earlier, 1.0, 0.0), axis=0, keepdims=True).astype(jnp.int32)


def exchange(dims, emb_hbm, lab_hbm, slab, frow, fpart, ans,
             emb, lab, send, stage, out, recv, other, khi, klo, qht, qlt, bias, part_sum,
             abuf, ay, ab, az,
             line_sem, load, gs, gr, fs, fr, ps, pr, ss, sr,
             nys, nyr, nzs, nzr, nxs, nxr, ncs, ncr, ays, ayr, azs, azr, axs, axr):
    Z, Y, X = dims
    nyz = Z * Y
    chips = nyz * X
    n_group = nyz // GROUP
    rows, width = emb.shape
    tiles = width // 128
    half_t = tiles // 2
    msg = 2 * tiles
    own = 2 * chips
    back = pow(STRIDE, -1, nyz)

    loads = [pltpu.make_async_copy(lab_hbm, lab, load.at[0])]
    part = rows // 4
    loads += [
        pltpu.make_async_copy(
            emb_hbm.at[pl.ds(i * part, part)], emb.at[pl.ds(i * part, part)], load.at[1 + i])
        for i in range(4)
    ]
    for copy in loads:
        copy.start()

    dp, x, core = position()
    yz = dp // 2
    y = yz % Y
    z = yz // Y
    me = x * nyz + yz
    zs = [(z + d) % Z for d in range(Z)]
    ys = [(y + d) % Y for d in range(Y)]
    partner = (yz * 2 + 1 - core, x)

    def at(dz, dy, dx=0):
        return ((zs[dz % Z] * Y + ys[dy % Y]) * 2 + core, (x + dx) % X)

    def signal(sem, where):
        pl.semaphore_signal(sem, inc=1, device_id=where, device_id_type=MESH)

    def start(src, dst, send_sem, recv_sem, where):
        pltpu.make_async_remote_copy(
            src_ref=src, dst_ref=dst, send_sem=send_sem, recv_sem=recv_sem,
            device_id=where, device_id_type=MESH,
        ).start()

    barrier = pltpu.get_barrier_semaphore()
    for d in range(1, Z):
        signal(barrier, at(d, 0))
    for d in range(1, Y):
        signal(barrier, at(0, d))
    for d in range(1, X):
        signal(barrier, at(0, 0, d))
    signal(barrier, partner)

    loads[0].wait()
    lrow = lab[...]
    rank = ranks(lrow)
    lx, lyz = lrow // nyz, lrow % nyz
    code = ((lyz // Y + Z - z) % Z) * Y + (lyz % Y + Y - y) % Y
    q_row = (code * back) % nyz
    target = 2 * (((q_row // GROUP) * X + (lx + X - x) % X) * GROUP + q_row % GROUP) + rank

    pl.semaphore_wait(barrier, Z + Y + X - 2)
    for d in range(1, Y):
        signal(line_sem, at(0, d))

    for copy in loads[1:]:
        copy.wait()
    e = emb[...]
    unit = e * lax.rsqrt(jnp.sum(e * e, axis=1, keepdims=True) + epsilon)
    parts = split3(unit)

    n_chunk = min(4, n_group)
    chunk = own // n_chunk
    chunk_q = nyz // n_chunk

    def fill(i):
        low = i * chunk
        place = jnp.where(iota((chunk, rows), 0) + low == target, 1.0, 0.0)
        filled = jnp.sum(place, axis=1, keepdims=True) > 0.5
        place = place.astype(bf16)
        slots = sum(jnp.dot(place, p, preferred_element_type=f32) for p in parts)
        slots = jnp.where(filled, slots, SENTINEL)
        for t in range(tiles):
            send[pl.ds(low * tiles + t, chunk, stride=tiles), :] = (
                slots[:, t * 128:(t + 1) * 128])

    def owner_at(q):
        w = (q * STRIDE) % nyz
        return ((z + w // Y) % Z * Y + (y + w % Y) % Y) * 2 + core, x

    def straight(q, carry):
        slot = (q // GROUP * X) * GROUP + q % GROUP
        start(send.at[pl.ds(slot * msg, msg)], recv.at[pl.ds(q * X * msg, msg)],
              fs, fr.at[q // GROUP], owner_at(q))
        return carry

    def onward(q, carry):
        piece = pl.ds((q * X + 1) * msg, (X - 1) * msg)
        start(out.at[piece], recv.at[piece], fs, fr.at[q // GROUP], owner_at(q))
        return carry

    block = GROUP * msg
    for i in range(n_chunk):
        fill(i)
        for g in range(i * chunk_q // GROUP, (i + 1) * chunk_q // GROUP):
            for dx in range(1, X):
                start(send.at[pl.ds((g * X + dx) * block, block)],
                      stage.at[pl.ds((g * (X - 1) + dx - 1) * block, block)],
                      gs, gr.at[g], at(0, 0, dx))
        if i == 0:
            pl.semaphore_wait(line_sem, Y - 1)
            recv[0:msg, :] = send[0:msg, :]
        lax.fori_loop(max(i * chunk_q, 1), (i + 1) * chunk_q, straight, 0)
    for g in range(n_group):
        wait_rows(stage, g * (X - 1) * block, (X - 1) * block, gr.at[g])
        for j in range(GROUP):
            q = g * GROUP + j
            into = recv if q == 0 else out
            for dx in range(1, X):
                into[pl.ds((q * X + dx) * msg, msg), :] = (
                    stage[pl.ds((g * (X - 1) + dx - 1) * block + j * msg, msg), :])
        lax.fori_loop(max(g * GROUP, 1), (g + 1) * GROUP, onward, 0)

    grows = GROUP * X * msg
    krows = GROUP * X * 2

    def take(buf, g, base, total):
        columns = []
        dead = None
        for t in range(tiles):
            v = buf[pl.ds(g * grows + t, krows, stride=tiles), :]
            if dead is None:
                dead = v > 2.0
                bias[pl.ds(base + g * krows, krows), :] = jnp.where(dead, -4.0, 0.0)
            v = jnp.where(dead, 0.0, v)
            hi = v.astype(bf16)
            lo = (v - hi.astype(f32)).astype(bf16)
            khi[pl.ds(base + g * krows, krows), t * 128:(t + 1) * 128] = hi
            klo[pl.ds(base + g * krows, krows), t * 128:(t + 1) * 128] = lo
            columns.append(jnp.sum(v, axis=0, keepdims=True))
        return total + jnp.concatenate(columns, axis=1)

    def take_own(g, total):
        total = take(recv, g, 0, total)
        have = (g + 1) * krows
        turn = 128 if own % 128 == 0 else krows
        if have % turn == 0:
            top = pl.ds(have - turn, turn)
            for t in range(tiles):
                lanes = pl.ds(t * 128, 128)
                qht[lanes, top] = khi[top, lanes].astype(f32).T.astype(bf16)
                qlt[lanes, top] = klo[top, lanes].astype(f32).T.astype(bf16)
        return total

    def take_other(g):
        wait_rows(other, g * grows, grows, pr.at[g])
        take(other, g, own, mine)

    mine = jnp.zeros((1, width), f32)
    for g in range(n_group):
        missing = X * msg if g == 0 else 0
        wait_rows(recv, g * grows + missing, grows - missing, fr.at[g])
        piece = pl.ds(g * grows, grows)
        start(recv.at[piece], other.at[piece], ps, pr.at[g], partner)
        if g > 0:
            mine = take_own(g - 1, mine)
        if g > 1:
            take_other(g - 2)
    mine = take_own(n_group - 1, mine)
    part_sum[0] = mine
    start(part_sum.at[0], part_sum.at[1], ss, sr, partner)
    for g in range(max(n_group - 2, 0), n_group):
        take_other(g)

    wait_rows(part_sum, 1, 1, sr)
    sums = mine + part_sum[1]
    fresh = sums * lax.rsqrt(jnp.sum(sums * sums, axis=1, keepdims=True) + epsilon)
    for t in range(half_t):
        a = fresh[:, t * 128:(t + 1) * 128]
        b = fresh[:, (half_t + t) * 128:(half_t + t + 1) * 128]
        frow[pl.ds(me * half_t + t, 1), :] = jnp.where(core == 0, a, b)
    piece = pl.ds(me * half_t, half_t)
    for d in range(1, Y):
        start(frow.at[piece], frow.at[piece], nys, nyr, at(0, d))
    fh = fresh.astype(bf16)
    khi[2 * own:2 * own + 16, :] = jnp.broadcast_to(fresh, (16, width)).astype(bf16)
    klo[2 * own:2 * own + 16, :] = jnp.broadcast_to(
        fresh - fh.astype(f32), (16, width)).astype(bf16)

    def product(first, count):
        kh = khi[first:first + count, :]
        kl = klo[first:first + count, :]
        dot = functools.partial(jnp.dot, preferred_element_type=f32)
        return dot(kh, qht[...]) + dot(kh, qlt[...]) + dot(kl, qht[...])

    def closest(s, first):
        off = bias[first:first + own, :]
        s = s + (jnp.concatenate([off] * (own // 128), axis=1) if own > 128 else off[:, :own])
        if first == 0:
            s = jnp.where(iota((own, own), 0) == iota((own, own), 1), -4.0, s)
        return jnp.max(s, axis=0, keepdims=True)

    best = jnp.maximum(closest(product(0, own), 0), -1.0)

    yrows = Y * half_t
    wait_rows(frow, 0, (Y - 1) * half_t, nyr)
    piece = pl.ds((x * nyz + z * Y) * half_t, yrows)
    for d in range(1, Z):
        start(frow.at[piece], frow.at[piece], nzs, nzr, at(d, 0))

    s = product(own, own + 16)
    best = jnp.maximum(best, closest(s[:own, :], own))
    cos = s[own:own + 1, :]

    xrows = nyz * half_t
    hrows = xrows // 2

    def block_of(dx, half):
        return pl.ds(((x + dx) % X) * xrows + half * hrows, hrows)

    def along(dx, half, sem, to):
        piece = block_of(dx, half)
        start(frow.at[piece], frow.at[piece], nxs, nxr.at[sem], at(0, 0, to))

    def pass_on(dx):
        piece = pl.ds(((x + dx) % X) * xrows, xrows)
        start(frow.at[piece], fpart.at[piece], ncs, ncr.at[dx], partner)

    def landed(dx, half, sem):
        wait_rows(frow, ((x + dx) % X) * xrows + half * hrows, hrows, nxr.at[sem])

    wait_rows(frow, 0, (Z - 1) * yrows, nzr)
    along(0, 0, 0, 1)
    if X > 2:
        along(0, 1, 2, X - 1)
    along(0, 1, 1, 1)
    if X > 2:
        along(0, 0, 3, X - 1)
    pass_on(0)
    xs = iota((128, own), 1) % (2 * X)
    lane_of = (xs // 2) * 8 + (xs % 2) * 2
    j = iota((128, own), 0)
    spread = jnp.where(j == lane_of, best, jnp.where(j == lane_of + 1, cos, 0.0))
    spread = jnp.sum(spread.T.reshape(nyz, 2 * X, 128), axis=1)
    for q in range(nyz):
        dz, dy = (q * STRIDE) % nyz // Y, (q * STRIDE) % nyz % Y
        abuf[dy * Z + dz:dy * Z + dz + 1, :] = spread[q:q + 1, :]
    for d in range(1, Y):
        start(abuf.at[pl.ds(d * Z, Z)], ay.at[pl.ds(y * Z, Z)], ays, ayr, at(0, -d))
    ay[pl.ds(y * Z, Z), :] = abuf[0:Z, :]

    if X > 2:
        landed(X - 1, 0, 0)
        along(X - 1, 0, 4, 1)
        landed(1, 1, 2)
        along(1, 1, 5, X - 1)

    wait_rows(ay, 0, (Y - 1) * Z, ayr)
    for dz in range(Z):
        ab[dz * Y:(dz + 1) * Y, :] = ay[pl.ds(dz, Y, stride=Z), :]
    for d in range(1, Z):
        start(ab.at[pl.ds(d * Y, Y)], az.at[pl.ds(z * Y, Y)], azs, azr, at(-d, 0))
    az[pl.ds(z * Y, Y), :] = ab[0:Y, :]

    if X > 2:
        landed(X - 1, 1, 1)
        pass_on(X - 1)
        landed(1, 0, 3)
        pass_on(1)
    else:
        landed(1, 0, 0)
        landed(1, 1, 1)
        pass_on(1)

    wait_rows(az, 0, (Z - 1) * Y, azr)
    wait_rows(ay, 0, (Y - 1) * Z, ays)
    turned = jnp.concatenate([az[...], jnp.zeros((128 - nyz, 128), f32)], axis=0).T
    abuf[0:8 * X, :] = turned[0:8 * X, :]
    for d in range(1, X):
        start(abuf.at[pl.ds(d * 8, 8)], ans.at[pl.ds(x * 8, 8)], axs, axr, at(0, 0, X - d))
    ans[pl.ds(x * 8, 8), :] = abuf[0:8, :]

    if X > 2:
        for half in range(2):
            landed(2, half, 4 + half)
            piece = block_of(2, half)
            start(frow.at[piece], fpart.at[piece], ncs, ncr.at[2 * (half + 1)], partner)
        for half in range(2):
            wait_rows(fpart, ((x + 2) % X) * xrows + half * hrows, hrows, ncr.at[2 * (half + 1)])
    for dx in range(X):
        if dx != 2:
            wait_rows(fpart, ((x + dx) % X) * xrows, xrows, ncr.at[dx])
    wait_rows(ans, 0, (X - 1) * 8, axr)

    wait_rows(send, 0, (X - 1) * nyz * msg, gs)
    wait_rows(send, 0, (nyz - 1) * X * msg, fs)
    wait_rows(part_sum, 0, 1, ss)
    wait_rows(recv, 0, n_group * grows, ps)
    wait_rows(frow, 0, (Y - 1) * half_t, nys)
    wait_rows(frow, 0, (Z - 1) * yrows, nzs)
    wait_rows(frow, 0, (X - 1) * xrows, nxs)
    wait_rows(frow, 0, X * xrows, ncs)
    wait_rows(az, 0, (Z - 1) * Y, azs)
    wait_rows(ans, 0, (X - 1) * 8, axs)


def finish(dims, frow, fpart, ans, lab, slab, cent, table_hbm, cos_hbm, sim_hbm,
           table, cos_out, sim_out, put):
    Z, Y, X = dims
    nyz = Z * Y
    chips = nyz * X
    trows, width = cent.shape
    half_t = width // 256
    dp, x, core = position()
    rows = lab.shape[1]

    low, high = [], []
    for t in range(half_t):
        a = frow[pl.ds(t, chips, stride=half_t), :]
        b = fpart[pl.ds(t, chips, stride=half_t), :]
        low.append(jnp.where(core == 0, a, b))
        high.append(jnp.where(core == 0, b, a))
    full = jnp.concatenate(low + high, axis=1)
    row_id = (dp * X + x) * trows + iota((trows, chips), 0)
    hit = jnp.where(row_id == slab[...], 1.0, 0.0)
    named = jnp.sum(hit, axis=1, keepdims=True) > 0.5
    table[...] = jnp.where(named, select_rows(hit.astype(bf16), full), cent[...])
    pairs = [(cos_out, cos_hbm), (sim_out, sim_hbm)]
    part = trows // 4
    pairs += [
        (table.at[pl.ds(i * part, part)], table_hbm.at[pl.ds(i * part, part)]) for i in range(4)]
    puts = [pltpu.make_async_copy(src, dst, put.at[i]) for i, (src, dst) in enumerate(pairs)]
    for copy in puts[2:]:
        copy.start()

    lrow = lab[...]
    rank = ranks(lrow)
    spot = (lrow // nyz) * 128 + lrow % nyz
    member = jnp.where(iota((X * 128, rows), 0) == spot, 1.0, 0.0).astype(bf16)
    got = jnp.concatenate([ans[i * 8:(i + 1) * 8, :] for i in range(X)], axis=1)
    got = jnp.concatenate([got, jnp.zeros_like(got)], axis=0)
    got = sum(jnp.dot(p, member, preferred_element_type=f32) for p in split3(got))
    sim_out[...] = jnp.where(rank == 0, got[0:1, :], got[2:3, :])
    cos_out[...] = jnp.where(rank == 0, got[1:2, :], got[3:4, :])
    puts[0].start()
    puts[1].start()
    for copy in puts:
        copy.wait()


def local(dims, embeddings, assignment, slab_ids, centroids):
    Z, Y, X = dims
    nyz = Z * Y
    chips = nyz * X
    rows, width = embeddings.shape
    tiles = width // 128
    n_group = nyz // GROUP
    linear = 2 * chips * tiles
    half = chips * tiles // 2
    dma = pltpu.SemaphoreType.DMA
    vmem = pl.BlockSpec(memory_space=pltpu.VMEM)
    hbm = pl.BlockSpec(memory_space=pl.ANY)
    shape = jax.ShapeDtypeStruct
    regular = pltpu.SemaphoreType.REGULAR
    labels = assignment.reshape(1, rows)
    slabs = slab_ids.reshape(1, chips)

    given = pl.pallas_call(
        functools.partial(exchange, dims),
        out_shape=(
            shape((half, 128), f32),
            shape((half, 128), f32),
            shape((8 * X, 128), f32),
        ),
        in_specs=[hbm] * 2 + [vmem],
        out_specs=(vmem,) * 3,
        scratch_shapes=[
            pltpu.VMEM((rows, width), f32),
            pltpu.VMEM((1, rows), jnp.int32),
            pltpu.VMEM((linear, 128), f32),
            pltpu.VMEM((linear // X * (X - 1), 128), f32),
            pltpu.VMEM((linear, 128), f32),
            pltpu.VMEM((linear, 128), f32),
            pltpu.VMEM((linear, 128), f32),
            pltpu.VMEM((4 * chips + 16, width), bf16),
            pltpu.VMEM((4 * chips + 16, width), bf16),
            pltpu.VMEM((width, 2 * chips), bf16),
            pltpu.VMEM((width, 2 * chips), bf16),
            pltpu.VMEM((4 * chips, 128), f32),
            pltpu.VMEM((2, 1, width), f32),
            pltpu.VMEM((max(nyz, 8 * X), 128), f32),
            pltpu.VMEM((nyz, 128), f32),
            pltpu.VMEM((nyz, 128), f32),
            pltpu.VMEM((nyz, 128), f32),
            regular,
            dma((5,)), dma, dma((n_group,)),
            dma, dma((n_group,)), dma, dma((n_group,)), dma, dma,
            dma, dma, dma, dma, dma, dma((6,)), dma, dma((X + 1,)),
            dma, dma, dma, dma, dma, dma,
        ],
        compiler_params=pltpu.CompilerParams(
            collective_id=0, has_side_effects=True, vmem_limit_bytes=KERNEL_BYTES),
    )(embeddings, labels, slabs)

    table, cos, sim = pl.pallas_call(
        functools.partial(finish, dims),
        out_shape=(
            shape(centroids.shape, f32),
            shape((1, rows), f32),
            shape((1, rows), f32),
        ),
        in_specs=[vmem] * 6,
        out_specs=(hbm,) * 3,
        scratch_shapes=[
            pltpu.VMEM(centroids.shape, f32),
            pltpu.VMEM((1, rows), f32),
            pltpu.VMEM((1, rows), f32),
            dma((6,)),
        ],
        compiler_params=pltpu.CompilerParams(vmem_limit_bytes=32 * 2**20),
    )(*given, labels, slabs, centroids)
    return table, cos.reshape(rows), sim.reshape(rows)


def solution(mesh, dims=(Z, Y, X)):
    placed = (P(("dp", "cent"), None), P(("dp", "cent"), None), P(), P(("dp", "cent"), None))
    return jax.shard_map(
        functools.partial(local, dims),
        mesh=mesh,
        in_specs=placed,
        out_specs=(P(("dp", "cent"), None), P(("dp", "cent")), P(("dp", "cent"))),
        check_vma=False,
    )
```

```python
import functools

import jax
import jax.numpy as jnp
from jax import lax
from jax.experimental import pallas as pl
from jax.experimental.pallas import tpu as pltpu
from jax.sharding import PartitionSpec as P

epsilon = 1e-06
Z, Y, X = 8, 8, 4
GROUP = 8
KERNEL_BYTES = 105 * 2**19
SENTINEL = 4.0
STRIDE = 37
MESH = pl.DeviceIdType.MESH
f32, bf16 = jnp.float32, jnp.bfloat16


def split3(v):
    hi = v.astype(bf16)
    rest = v - hi.astype(f32)
    mid = rest.astype(bf16)
    lo = (rest - mid.astype(f32)).astype(bf16)
    return hi, mid, lo


def select_rows(onehot, v):
    hi, mid, lo = split3(v)
    dot = functools.partial(jnp.dot, preferred_element_type=f32)
    return dot(onehot, hi) + dot(onehot, mid) + dot(onehot, lo)


def iota(shape, axis):
    return lax.broadcasted_iota(jnp.int32, shape, axis)


def position():
    dp = lax.axis_index("dp")
    return dp, lax.axis_index("cent"), dp % 2


def wait_rows(buf, start, count, sem):
    part = buf.at[pl.ds(start, count)]
    pltpu.make_async_copy(part, part, sem).wait()


def ranks(lrow):
    rows = lrow.shape[1]
    lcol = jnp.broadcast_to(lrow.astype(f32), (128, rows)).T[:, 0:1].astype(jnp.int32)
    earlier = (lcol == lrow) & (iota((rows, rows), 0) < iota((rows, rows), 1))
    return jnp.sum(jnp.where(earlier, 1.0, 0.0), axis=0, keepdims=True).astype(jnp.int32)


def exchange(dims, emb_hbm, lab_hbm, slab, frow, fpart, ans,
             emb, lab, send, recv, other, khi, klo, qht, qlt, bias, part_sum,
             abuf, ay, ab, az,
             line_sem, plane_sem, load, fs, fr, ps, pr, ss, sr,
             nys, nyr, nzs, nzr, nxs, nxr, ncs, ncr, ays, ayr, azs, azr, axs, axr):
    Z, Y, X = dims
    nyz = Z * Y
    chips = nyz * X
    n_group = nyz // GROUP
    rows, width = emb.shape
    tiles = width // 128
    half_t = tiles // 2
    msg = 2 * tiles
    own = 2 * chips
    back = pow(STRIDE, -1, nyz)

    loads = [pltpu.make_async_copy(lab_hbm, lab, load.at[0])]
    part = rows // 4
    loads += [
        pltpu.make_async_copy(
            emb_hbm.at[pl.ds(i * part, part)], emb.at[pl.ds(i * part, part)], load.at[1 + i])
        for i in range(4)
    ]
    for copy in loads:
        copy.start()

    dp, x, core = position()
    yz = dp // 2
    y = yz % Y
    z = yz // Y
    me = x * nyz + yz
    zs = [(z + d) % Z for d in range(Z)]
    ys = [(y + d) % Y for d in range(Y)]
    partner = (yz * 2 + 1 - core, x)

    def at(dz, dy, dx=0):
        return ((zs[dz % Z] * Y + ys[dy % Y]) * 2 + core, (x + dx) % X)

    def signal(sem, where):
        pl.semaphore_signal(sem, inc=1, device_id=where, device_id_type=MESH)

    def start(src, dst, send_sem, recv_sem, where):
        pltpu.make_async_remote_copy(
            src_ref=src, dst_ref=dst, send_sem=send_sem, recv_sem=recv_sem,
            device_id=where, device_id_type=MESH,
        ).start()

    barrier = pltpu.get_barrier_semaphore()
    for d in range(1, Z):
        signal(barrier, at(d, 0))
    for d in range(1, Y):
        signal(barrier, at(0, d))
    for d in range(1, X):
        signal(barrier, at(0, 0, d))
    signal(barrier, partner)

    loads[0].wait()
    lrow = lab[...]
    rank = ranks(lrow)
    lx, lyz = lrow // nyz, lrow % nyz
    code = ((lyz // Y + Z - z) % Z) * Y + (lyz % Y + Y - y) % Y
    target = 2 * (((code * back) % nyz) * X + (lx + X - x) % X) + rank

    pl.semaphore_wait(barrier, Z + Y + X - 2)
    for d in range(1, Y):
        signal(line_sem, at(0, d))

    for copy in loads[1:]:
        copy.wait()
    e = emb[...]
    unit = e * lax.rsqrt(jnp.sum(e * e, axis=1, keepdims=True) + epsilon)
    parts = split3(unit)

    n_chunk = min(4, n_group)
    chunk = own // n_chunk
    chunk_q = nyz // n_chunk

    def fill(i):
        low = i * chunk
        place = jnp.where(iota((chunk, rows), 0) + low == target, 1.0, 0.0)
        filled = jnp.sum(place, axis=1, keepdims=True) > 0.5
        place = place.astype(bf16)
        slots = sum(jnp.dot(place, p, preferred_element_type=f32) for p in parts)
        slots = jnp.where(filled, slots, SENTINEL)
        for t in range(tiles):
            send[pl.ds(low * tiles + t, chunk, stride=tiles), :] = (
                slots[:, t * 128:(t + 1) * 128])

    def straight(q, dx):
        w = (q * STRIDE) % nyz
        where = (((z + w // Y) % Z * Y + (y + w % Y) % Y) * 2 + core, (x + dx) % X)
        piece = pl.ds((q * X + dx) * msg, msg)
        start(send.at[piece], recv.at[piece], fs, fr.at[q // GROUP], where)

    def straight_all(first, last, dxs):
        def step(q, carry):
            for dx in dxs:
                straight(q, dx)
            return carry
        lax.fori_loop(first, last, step, 0)

    fill(0)
    pl.semaphore_wait(line_sem, Y - 1)
    for d in range(1, X):
        signal(plane_sem, at(0, 0, d))
    straight_all(1, chunk_q, [0])
    recv[0:msg, :] = send[0:msg, :]
    fill(1)
    pl.semaphore_wait(plane_sem, X - 1)
    straight_all(0, chunk_q, range(1, X))
    for i in range(1, n_chunk):
        if i > 1:
            fill(i)
        straight_all(i * chunk_q, (i + 1) * chunk_q, range(X))

    grows = GROUP * X * msg
    krows = GROUP * X * 2

    def take(buf, g, base, total):
        columns = []
        dead = None
        for t in range(tiles):
            v = buf[pl.ds(g * grows + t, krows, stride=tiles), :]
            if dead is None:
                dead = v > 2.0
                bias[pl.ds(base + g * krows, krows), :] = jnp.where(dead, -4.0, 0.0)
            v = jnp.where(dead, 0.0, v)
            hi = v.astype(bf16)
            lo = (v - hi.astype(f32)).astype(bf16)
            khi[pl.ds(base + g * krows, krows), t * 128:(t + 1) * 128] = hi
            klo[pl.ds(base + g * krows, krows), t * 128:(t + 1) * 128] = lo
            columns.append(jnp.sum(v, axis=0, keepdims=True))
        return total + jnp.concatenate(columns, axis=1)

    def take_own(g, total):
        total = take(recv, g, 0, total)
        have = (g + 1) * krows
        turn = 128 if own % 128 == 0 else krows
        if have % turn == 0:
            top = pl.ds(have - turn, turn)
            for t in range(tiles):
                lanes = pl.ds(t * 128, 128)
                qht[lanes, top] = khi[top, lanes].astype(f32).T.astype(bf16)
                qlt[lanes, top] = klo[top, lanes].astype(f32).T.astype(bf16)
        return total

    def take_other(g):
        wait_rows(other, g * grows, grows, pr.at[g])
        take(other, g, own, mine)

    mine = jnp.zeros((1, width), f32)
    for g in range(n_group):
        missing = msg if g == 0 else 0
        wait_rows(recv, g * grows + missing, grows - missing, fr.at[g])
        piece = pl.ds(g * grows, grows)
        start(recv.at[piece], other.at[piece], ps, pr.at[g], partner)
        mine = take_own(g, mine)
        if g < n_group - 1:
            take_other(g)
    part_sum[0] = mine
    start(part_sum.at[0], part_sum.at[1], ss, sr, partner)
    take_other(n_group - 1)

    wait_rows(part_sum, 1, 1, sr)
    sums = mine + part_sum[1]
    fresh = sums * lax.rsqrt(jnp.sum(sums * sums, axis=1, keepdims=True) + epsilon)
    for t in range(half_t):
        a = fresh[:, t * 128:(t + 1) * 128]
        b = fresh[:, (half_t + t) * 128:(half_t + t + 1) * 128]
        frow[pl.ds(me * half_t + t, 1), :] = jnp.where(core == 0, a, b)
    piece = pl.ds(me * half_t, half_t)
    for d in range(1, Y):
        start(frow.at[piece], frow.at[piece], nys, nyr, at(0, d))
    fh = fresh.astype(bf16)
    khi[2 * own:2 * own + 16, :] = jnp.broadcast_to(fresh, (16, width)).astype(bf16)
    klo[2 * own:2 * own + 16, :] = jnp.broadcast_to(
        fresh - fh.astype(f32), (16, width)).astype(bf16)

    def product(first, count):
        kh = khi[first:first + count, :]
        kl = klo[first:first + count, :]
        dot = functools.partial(jnp.dot, preferred_element_type=f32)
        return dot(kh, qht[...]) + dot(kh, qlt[...]) + dot(kl, qht[...])

    def closest(s, first):
        off = bias[first:first + own, :]
        s = s + (jnp.concatenate([off] * (own // 128), axis=1) if own > 128 else off[:, :own])
        if first == 0:
            s = jnp.where(iota((own, own), 0) == iota((own, own), 1), -4.0, s)
        return jnp.max(s, axis=0, keepdims=True)

    best = jnp.maximum(closest(product(0, own), 0), -1.0)

    yrows = Y * half_t
    wait_rows(frow, 0, (Y - 1) * half_t, nyr)
    piece = pl.ds((x * nyz + z * Y) * half_t, yrows)
    for d in range(1, Z):
        start(frow.at[piece], frow.at[piece], nzs, nzr, at(d, 0))

    s = product(own, own + 16)
    best = jnp.maximum(best, closest(s[:own, :], own))
    cos = s[own:own + 1, :]

    xs = iota((128, own), 1) % (2 * X)
    lane_of = (xs // 2) * 8 + (xs % 2) * 2
    j = iota((128, own), 0)
    spread = jnp.where(j == lane_of, best, jnp.where(j == lane_of + 1, cos, 0.0))
    spread = jnp.sum(spread.T.reshape(nyz, 2 * X, 128), axis=1)
    for q in range(nyz):
        dz, dy = (q * STRIDE) % nyz // Y, (q * STRIDE) % nyz % Y
        abuf[dy * Z + dz:dy * Z + dz + 1, :] = spread[q:q + 1, :]
    for d in range(1, Y):
        start(abuf.at[pl.ds(d * Z, Z)], ay.at[pl.ds(y * Z, Z)], ays, ayr, at(0, -d))
    ay[pl.ds(y * Z, Z), :] = abuf[0:Z, :]

    xrows = nyz * half_t
    hrows = xrows // 2

    def block_of(dx, half):
        return pl.ds(((x + dx) % X) * xrows + half * hrows, hrows)

    def along(dx, half, sem, to):
        piece = block_of(dx, half)
        start(frow.at[piece], frow.at[piece], nxs, nxr.at[sem], at(0, 0, to))

    def pass_on(dx):
        piece = pl.ds(((x + dx) % X) * xrows, xrows)
        start(frow.at[piece], fpart.at[piece], ncs, ncr.at[dx], partner)

    def landed(dx, half, sem):
        wait_rows(frow, ((x + dx) % X) * xrows + half * hrows, hrows, nxr.at[sem])

    wait_rows(frow, 0, (Z - 1) * yrows, nzr)
    along(0, 0, 0, 1)
    if X > 2:
        along(0, 1, 2, X - 1)
    along(0, 1, 1, 1)
    if X > 2:
        along(0, 0, 3, X - 1)
    pass_on(0)
    wait_rows(ay, 0, (Y - 1) * Z, ayr)
    for dz in range(Z):
        ab[dz * Y:(dz + 1) * Y, :] = ay[pl.ds(dz, Y, stride=Z), :]
    for d in range(1, Z):
        start(ab.at[pl.ds(d * Y, Y)], az.at[pl.ds(z * Y, Y)], azs, azr, at(-d, 0))
    az[pl.ds(z * Y, Y), :] = ab[0:Y, :]

    if X > 2:
        landed(X - 1, 0, 0)
        along(X - 1, 0, 4, 1)
        landed(1, 1, 2)
        along(1, 1, 5, X - 1)

    wait_rows(az, 0, (Z - 1) * Y, azr)
    wait_rows(ay, 0, (Y - 1) * Z, ays)
    turned = jnp.concatenate([az[...], jnp.zeros((128 - nyz, 128), f32)], axis=0).T
    abuf[0:8 * X, :] = turned[0:8 * X, :]
    for d in range(1, X):
        start(abuf.at[pl.ds(d * 8, 8)], ans.at[pl.ds(x * 8, 8)], axs, axr, at(0, 0, X - d))
    ans[pl.ds(x * 8, 8), :] = abuf[0:8, :]

    if X > 2:
        landed(X - 1, 1, 1)
        pass_on(X - 1)
        landed(1, 0, 3)
        pass_on(1)
    else:
        landed(1, 0, 0)
        landed(1, 1, 1)
        pass_on(1)

    if X > 2:
        for side in range(2):
            landed(2, side, 4 + side)
            piece = block_of(2, side)
            start(frow.at[piece], fpart.at[piece], ncs, ncr.at[2 * (side + 1)], partner)
        for side in range(2):
            wait_rows(fpart, ((x + 2) % X) * xrows + side * hrows, hrows, ncr.at[2 * (side + 1)])
    for dx in range(X):
        if dx != 2:
            wait_rows(fpart, ((x + dx) % X) * xrows, xrows, ncr.at[dx])
    wait_rows(ans, 0, (X - 1) * 8, axr)

    wait_rows(send, 0, (chips - 1) * msg, fs)
    wait_rows(part_sum, 0, 1, ss)
    wait_rows(recv, 0, n_group * grows, ps)
    wait_rows(frow, 0, (Y - 1) * half_t, nys)
    wait_rows(frow, 0, (Z - 1) * yrows, nzs)
    wait_rows(frow, 0, (X - 1) * xrows, nxs)
    wait_rows(frow, 0, X * xrows, ncs)
    wait_rows(az, 0, (Z - 1) * Y, azs)
    wait_rows(ans, 0, (X - 1) * 8, axs)


def finish(dims, frow, fpart, ans, lab, slab, cent, table_hbm, cos_hbm, sim_hbm,
           table, cos_out, sim_out, put):
    Z, Y, X = dims
    nyz = Z * Y
    chips = nyz * X
    trows, width = cent.shape
    half_t = width // 256
    dp, x, core = position()
    rows = lab.shape[1]

    low, high = [], []
    for t in range(half_t):
        a = frow[pl.ds(t, chips, stride=half_t), :]
        b = fpart[pl.ds(t, chips, stride=half_t), :]
        low.append(jnp.where(core == 0, a, b))
        high.append(jnp.where(core == 0, b, a))
    full = jnp.concatenate(low + high, axis=1)
    row_id = (dp * X + x) * trows + iota((trows, chips), 0)
    hit = jnp.where(row_id == slab[...], 1.0, 0.0)
    named = jnp.sum(hit, axis=1, keepdims=True) > 0.5
    table[...] = jnp.where(named, select_rows(hit.astype(bf16), full), cent[...])
    pairs = [(cos_out, cos_hbm), (sim_out, sim_hbm)]
    part = trows // 4
    pairs += [
        (table.at[pl.ds(i * part, part)], table_hbm.at[pl.ds(i * part, part)]) for i in range(4)]
    puts = [pltpu.make_async_copy(src, dst, put.at[i]) for i, (src, dst) in enumerate(pairs)]
    for copy in puts[2:]:
        copy.start()

    lrow = lab[...]
    rank = ranks(lrow)
    spot = (lrow // nyz) * 128 + lrow % nyz
    member = jnp.where(iota((X * 128, rows), 0) == spot, 1.0, 0.0).astype(bf16)
    got = jnp.concatenate([ans[i * 8:(i + 1) * 8, :] for i in range(X)], axis=1)
    got = jnp.concatenate([got, jnp.zeros_like(got)], axis=0)
    got = sum(jnp.dot(p, member, preferred_element_type=f32) for p in split3(got))
    sim_out[...] = jnp.where(rank == 0, got[0:1, :], got[2:3, :])
    cos_out[...] = jnp.where(rank == 0, got[1:2, :], got[3:4, :])
    puts[0].start()
    puts[1].start()
    for copy in puts:
        copy.wait()


def local(dims, embeddings, assignment, slab_ids, centroids):
    Z, Y, X = dims
    nyz = Z * Y
    chips = nyz * X
    rows, width = embeddings.shape
    tiles = width // 128
    n_group = nyz // GROUP
    linear = 2 * chips * tiles
    half = chips * tiles // 2
    dma = pltpu.SemaphoreType.DMA
    vmem = pl.BlockSpec(memory_space=pltpu.VMEM)
    hbm = pl.BlockSpec(memory_space=pl.ANY)
    shape = jax.ShapeDtypeStruct
    regular = pltpu.SemaphoreType.REGULAR
    labels = assignment.reshape(1, rows)
    slabs = slab_ids.reshape(1, chips)

    given = pl.pallas_call(
        functools.partial(exchange, dims),
        out_shape=(
            shape((half, 128), f32),
            shape((half, 128), f32),
            shape((8 * X, 128), f32),
        ),
        in_specs=[hbm] * 2 + [vmem],
        out_specs=(vmem,) * 3,
        scratch_shapes=[
            pltpu.VMEM((rows, width), f32),
            pltpu.VMEM((1, rows), jnp.int32),
            pltpu.VMEM((linear, 128), f32),
            pltpu.VMEM((linear, 128), f32),
            pltpu.VMEM((linear, 128), f32),
            pltpu.VMEM((4 * chips + 16, width), bf16),
            pltpu.VMEM((4 * chips + 16, width), bf16),
            pltpu.VMEM((width, 2 * chips), bf16),
            pltpu.VMEM((width, 2 * chips), bf16),
            pltpu.VMEM((4 * chips, 128), f32),
            pltpu.VMEM((2, 1, width), f32),
            pltpu.VMEM((max(nyz, 8 * X), 128), f32),
            pltpu.VMEM((nyz, 128), f32),
            pltpu.VMEM((nyz, 128), f32),
            pltpu.VMEM((nyz, 128), f32),
            regular, regular,
            dma((5,)),
            dma, dma((n_group,)), dma, dma((n_group,)), dma, dma,
            dma, dma, dma, dma, dma, dma((6,)), dma, dma((X + 1,)),
            dma, dma, dma, dma, dma, dma,
        ],
        compiler_params=pltpu.CompilerParams(
            collective_id=0, has_side_effects=True, vmem_limit_bytes=KERNEL_BYTES),
    )(embeddings, labels, slabs)

    table, cos, sim = pl.pallas_call(
        functools.partial(finish, dims),
        out_shape=(
            shape(centroids.shape, f32),
            shape((1, rows), f32),
            shape((1, rows), f32),
        ),
        in_specs=[vmem] * 6,
        out_specs=(hbm,) * 3,
        scratch_shapes=[
            pltpu.VMEM(centroids.shape, f32),
            pltpu.VMEM((1, rows), f32),
            pltpu.VMEM((1, rows), f32),
            dma((6,)),
        ],
        compiler_params=pltpu.CompilerParams(vmem_limit_bytes=32 * 2**20),
    )(*given, labels, slabs, centroids)
    return table, cos.reshape(rows), sim.reshape(rows)


def solution(mesh, dims=(Z, Y, X)):
    placed = (P(("dp", "cent"), None), P(("dp", "cent"), None), P(), P(("dp", "cent"), None))
    return jax.shard_map(
        functools.partial(local, dims),
        mesh=mesh,
        in_specs=placed,
        out_specs=(P(("dp", "cent"), None), P(("dp", "cent")), P(("dp", "cent"))),
        check_vma=False,
    )
```
